256 devices in a mesh: grp: 16 (over z, core), mem: 16 (over x, y).
Axes of the slice: x: 4, y: 4, z: 8, core: 2. Of those that a mesh axis runs over, the one named last changes fastest.
Arguments:
- tokens: bfloat16 [16384, 1024], P(('grp', 'mem')), may hold values from -6 to 6
- in_weight: bfloat16 [1024, 4096], replicated, may hold values from -0.1875 to 0.1875
- out_weight: bfloat16 [1024, 1024], replicated, may hold values from -0.1875 to 0.1875
- history_pool: bfloat16 [224, 512, 2048], P('grp', 'mem'), may hold values from -6 to 6
- position_bias: float32 [8, 14], replicated, may hold values from -2 to 2
- self_bias: float32 [8], replicated, may hold values from 2 to 6
- history_length: int32 [16], P('grp'), may hold values from 5633 to 7168, as said below
- candidate_count: int32 [16], P('grp'), may hold values from 256 to 1024, as said below
- block_slots: int32 [16, 16, 2], P('grp'), may hold values from -1 to 13, as said below
- block_position: int32 [16, 16, 2], P('grp'), may hold values from -1 to 13, as said below
Outputs:
- scored: bfloat16 [16384, 1024], P(('grp', 'mem'))
The draws below stay inside these ranges and needn't reach their ends.
Inputs may be any that keep to these rules, and one draw needn't show every extreme that they name: `history_length`: the group with the longest history reaches 7168 tokens. `candidate_count`: some group has all 1024 slots real. `block_slots`: entries are indices into the 14 blocks owned by group o, or -1 for an empty slot; every pool block is listed at most once; at most 2 blocks go from one owner group to one scoring group, and in every draw some owner sends exactly 2; a group reads at most 14 blocks, and some group reads exactly 14. `block_position`: -1 exactly where block_slots is -1; for group d the positions 0 to ceil(history_length[d] / 512) - 1 each appear exactly once and no others.
All inputs are finite; a program needn't handle non-finite values.
Results may differ from the reference program's by a relative error of at most 0.014.
Values may be sent and summed in bfloat16 or wider, within the bound.
No kernel may reach another device: no remote copies, remote signals or barrier semaphores. Data moves between devices by JAX's collectives and lax.ppermute only.
A program may use at most 128 MiB of HBM per device.

```python
import math
import jax
import jax.numpy as jnp
from jax import lax

D = 1024
HEADS = 8
HEAD = 128
CAND = 1024
BLOCK = 512
BLK_REQ = 14
CAP = 2
POOL = 224
TOKENS = 16384
N_GRP = 16


def layout(key):
    first_key, second_key, third_key, fourth_key, fifth_key = jax.random.split(key, 5)
    group_ids = jnp.arange(N_GRP, dtype=jnp.int32)
    block_ids = jnp.arange(BLK_REQ, dtype=jnp.int32)
    counts = jax.random.randint(first_key, (N_GRP,), BLK_REQ - BLK_REQ // 5, BLK_REQ + 1)
    busiest = jax.random.randint(second_key, (), 0, N_GRP)
    counts = jnp.where(group_ids == busiest, BLK_REQ, counts).astype(jnp.int32)
    order_scores = jax.random.randint(third_key, (N_GRP, BLK_REQ), 0, 1 << 20) * BLK_REQ + block_ids[None, :]
    shuffled = jnp.argsort(order_scores, axis=1).astype(jnp.int32)
    group_scores = jax.random.randint(fourth_key, (N_GRP,), 0, 1 << 20) * N_GRP + group_ids
    circle = jnp.argsort(group_scores).astype(jnp.int32)
    placing = jnp.argsort(circle).astype(jnp.int32)
    local_scores = jax.random.randint(fifth_key, (N_GRP, BLK_REQ), 0, 1 << 20) * BLK_REQ + block_ids[None, :]
    local_scores = jnp.where(block_ids[None, :] == 0, (1 << 20) * BLK_REQ + BLK_REQ, local_scores)
    relabel = jnp.argsort(jnp.argsort(local_scores, axis=1), axis=1).astype(jnp.int32)
    destination = jnp.broadcast_to(group_ids[:, None], (N_GRP, BLK_REQ))
    quotient = shuffled // CAP
    remainder = shuffled % CAP
    owner = circle[(placing[destination] + quotient) % N_GRP]
    local_block = relabel[owner, shuffled]
    valid = block_ids[None, :] < counts[:, None]
    position_grid = jnp.broadcast_to(block_ids[None, :], (N_GRP, BLK_REQ))
    empty = jnp.full((N_GRP, N_GRP, CAP), -1, jnp.int32)
    slot_table = empty.at[destination, owner, remainder].set(jnp.where(valid, local_block, -1))
    position_table = empty.at[destination, owner, remainder].set(jnp.where(valid, position_grid, -1))
    return (counts, busiest, slot_table, position_table)


def draw_history_length(key, part):
    drawn = layout(key)
    key = jax.random.fold_in(key, 1)
    counts = drawn[0]
    busiest = drawn[1]
    extra = jax.random.randint(key, (N_GRP,), 1, BLOCK + 1)
    extra = jnp.where(jnp.arange(N_GRP, dtype=jnp.int32) == busiest, BLOCK, extra)
    return ((counts - 1) * BLOCK + extra).astype(jnp.int32)


def draw_candidate_count(key, part):
    key = jax.random.fold_in(key, 2)
    first_key, second_key = jax.random.split(key, 2)
    counts = jax.random.randint(first_key, (N_GRP,), CAND // 4, CAND + 1)
    fullest = jax.random.randint(second_key, (), 0, N_GRP)
    return jnp.where(jnp.arange(N_GRP, dtype=jnp.int32) == fullest, CAND, counts).astype(jnp.int32)


def draw_block_slots(key, part):
    drawn = layout(key)
    return drawn[2]


def draw_block_position(key, part):
    drawn = layout(key)
    return drawn[3]


def steps_of(key, dims, pieces, smallest, top_value):
    gain, own = 1.0, jax.random.fold_in(key, 6)
    for position, shards_of in pieces:
        heights = jnp.exp(jax.random.uniform(jax.random.fold_in(own, position), (shards_of,), jnp.float32, smallest / len(pieces), top_value / len(pieces)))
        gain = gain * jnp.repeat(heights, dims[position] // shards_of).reshape([-1 if axis == position else 1 for axis in range(len(dims))])
    return gain


def noise(rng, shape, scale, bound, shards=(), held_as=jnp.bfloat16):
    gain = steps_of(rng, shape, shards, -0.22, 0.18) if shards else 1.0
    values = jax.random.normal(rng, shape, jnp.float32) * scale * gain
    return jnp.minimum(jnp.maximum(values, -bound), bound).astype(held_as)


def setup_inputs(seed: int = 0) -> dict:
    splits = jax.random.split(jax.random.key(seed), 11)
    tokens = noise(splits[0], (TOKENS, D), 1.0, 6.0, ((0, 256),))
    in_weight = noise(splits[1], (D, 4 * D), D ** -0.5, 0.1875)
    out_weight = noise(splits[2], (D, D), D ** -0.5, 0.1875)
    history_pool = noise(splits[3], (POOL, BLOCK, 2 * D), 1.0, 6.0, ((0, 16), (1, 16)))
    position_bias = jnp.clip(jax.random.uniform(splits[4], (HEADS, BLK_REQ), jnp.float32, -2.0, 2.0), -2.0, 2.0)
    self_bias = jnp.clip(jnp.exp(jax.random.uniform(splits[5], (HEADS,), jnp.float32, math.log(2.0), math.log(6.0))), 2.0, 6.0)
    history_length = draw_history_length(jax.random.fold_in(splits[10], 71), 0)
    candidate_count = draw_candidate_count(jax.random.fold_in(splits[10], 71), 0)
    block_slots = draw_block_slots(jax.random.fold_in(splits[10], 71), 0)
    block_position = draw_block_position(jax.random.fold_in(splits[10], 71), 0)
    return {"tokens": tokens, "in_weight": in_weight, "out_weight": out_weight, "history_pool": history_pool, "position_bias": position_bias, "self_bias": self_bias, "history_length": history_length, "candidate_count": candidate_count, "block_slots": block_slots, "block_position": block_position}


epsilon = 1e-05

def layer_norm(values):
    center = values - lax.optimization_barrier(jnp.mean(values, axis=-1, keepdims=True))
    spread = lax.optimization_barrier(jnp.mean(center * center, axis=-1, keepdims=True))
    return center * lax.rsqrt(spread + epsilon)

def project(tokens, in_weight):
    normed = layer_norm(tokens.astype(jnp.float32)).astype(jnp.bfloat16)
    projected = jax.nn.silu(jnp.dot(normed, in_weight, preferred_element_type=jnp.float32))
    quarters = jnp.split(projected, 4, axis=1)
    return tuple((quarter.astype(jnp.bfloat16) for quarter in quarters))

def reference(tokens, in_weight, out_weight, history_pool, position_bias, self_bias, history_length, candidate_count, block_slots, block_position):
    score_scale = HEAD ** (-0.5)

    def one_group(group_index):
        rows_here = lax.dynamic_slice_in_dim(tokens, group_index * CAND, CAND, 0)
        gate_u, value_v, query_rows, key_new = project(rows_here, in_weight)
        slots_here = block_slots[group_index]
        positions = block_position[group_index].reshape(-1)
        pool_index = (jnp.arange(N_GRP, dtype=jnp.int32)[:, None] * BLK_REQ + jnp.clip(slots_here, 0, BLK_REQ - 1)).reshape(-1)
        matches = positions[None, :] == jnp.arange(BLK_REQ, dtype=jnp.int32)[:, None]
        present = jnp.any(matches, axis=1)
        chosen = lax.optimization_barrier(jnp.sum(jnp.where(matches, pool_index[None, :], 0), axis=1)).astype(jnp.int32)
        history = history_pool[chosen].reshape(BLK_REQ * BLOCK, 2 * D)
        token_index = jnp.arange(BLK_REQ * BLOCK, dtype=jnp.int32)
        block_of = token_index // BLOCK
        live_mask = (present[block_of] & (token_index < history_length[group_index])).astype(jnp.float32)
        head_terms = []
        for head_index in range(HEADS):
            low_col = head_index * HEAD
            high_col = low_col + HEAD
            scores = jnp.dot(query_rows[:, low_col:high_col], history[:, low_col:high_col].T, preferred_element_type=jnp.float32)
            bias_row = position_bias[head_index][block_of]
            weights = (jax.nn.silu(scores * score_scale + bias_row[None, :]) * live_mask[None, :]).astype(jnp.bfloat16)
            hist_term = jnp.dot(weights, history[:, D + low_col:D + high_col], preferred_element_type=jnp.float32)
            self_score = lax.optimization_barrier(jnp.sum(query_rows[:, low_col:high_col].astype(jnp.float32) * key_new[:, low_col:high_col].astype(jnp.float32), axis=1)) * score_scale + self_bias[head_index]
            head_terms.append(hist_term + jax.nn.silu(self_score)[:, None] * value_v[:, low_col:high_col].astype(jnp.float32))
        attended = jnp.concatenate(head_terms, axis=1)
        gated = (layer_norm(attended) * gate_u.astype(jnp.float32)).astype(jnp.bfloat16)
        output = jnp.dot(gated, out_weight, preferred_element_type=jnp.float32) + rows_here.astype(jnp.float32)
        row_index = jnp.arange(CAND, dtype=jnp.int32)
        return jnp.where(row_index[:, None] < candidate_count[group_index], output, 0.0).astype(jnp.bfloat16)
    scored = lax.map(one_group, jnp.arange(N_GRP, dtype=jnp.int32))
    return scored.reshape(N_GRP * CAND, D)
```

```python
import jax
import jax.numpy as jnp
from jax import lax
from jax.experimental import pallas as pl
from jax.experimental.pallas import tpu as pltpu
from jax.sharding import Mesh, PartitionSpec as P

D = 1024
HEADS = 8
HEAD = 128
BLOCK = 512
BLK = 14
CAP = 2
NZ = 8
NG = 16
NM = 16
SLAB = 32
ROWS = 64
HALF = 512
EPS = 1e-05
SCALE = HEAD**-0.5
G = ("z", "core")
M = ("x", "y")
VM = pl.BlockSpec(memory_space=pltpu.VMEM)
SM = pl.BlockSpec(memory_space=pltpu.SMEM)
ANY = pl.BlockSpec(memory_space=pl.ANY)


def params(mib):
    return pltpu.CompilerParams(vmem_limit_bytes=mib << 20)


def norm(values):
    center = values - jnp.mean(values, axis=-1, keepdims=True)
    spread = jnp.mean(center * center, axis=-1, keepdims=True)
    return center * lax.rsqrt(spread + EPS)


def silu(v):
    t = 0.5 * v
    return t + t * jnp.tanh(t)


def pack_kernel(pool, out, sems):
    copies = []
    for h in range(HEADS):
        for kv in range(2):
            for ch in range(2):
                copies.append(
                    pltpu.make_async_copy(
                        pool.at[:, :, pl.ds(kv * D + h * HEAD, HEAD)],
                        out.at[h * 2 + ch, kv],
                        sems.at[(h * 2 + kv) * 2 + ch],
                    )
                )
    for c in copies:
        c.start()
    for c in copies:
        c.wait()


def pack(pool):
    return pl.pallas_call(
        pack_kernel,
        out_shape=jax.ShapeDtypeStruct((NM, 2, BLK, SLAB, HEAD), jnp.bfloat16),
        in_specs=[ANY],
        out_specs=ANY,
        scratch_shapes=[pltpu.SemaphoreType.DMA((32,))],
        name="pack_history",
    )(pool)


def query_kernel(tokens, w, q_out, send_out):
    h2 = pl.program_id(0)
    normed = norm(tokens[...].astype(jnp.float32)).astype(jnp.bfloat16)
    q = silu(jnp.dot(normed, w[...], preferred_element_type=jnp.float32)).astype(jnp.bfloat16)
    q_out[...] = q
    for j in range(2):
        for ch in range(2):
            send_out[j * 2 + ch] = q[ch * 32 : ch * 32 + 32, j * HEAD : (j + 1) * HEAD]


def query(tokens, w):
    return pl.pallas_call(
        query_kernel,
        grid=(4,),
        out_shape=(
            jax.ShapeDtypeStruct((ROWS, D), jnp.bfloat16),
            jax.ShapeDtypeStruct((NM, 32, HEAD), jnp.bfloat16),
        ),
        in_specs=[
            pl.BlockSpec((ROWS, D), lambda i: (0, 0)),
            pl.BlockSpec((D, 256), lambda i: (0, 8 + i)),
        ],
        out_specs=(
            pl.BlockSpec((ROWS, 256), lambda i: (0, i)),
            pl.BlockSpec((4, 32, HEAD), lambda i: (i, 0, 0)),
        ),
        compiler_params=params(16),
        name="project_query",
    )(tokens, w)


def rest_kernel(tokens, wu, wv, wk, q, self_bias, gate_out, self_out):
    i = pl.program_id(0)
    normed = norm(tokens[...].astype(jnp.float32)).astype(jnp.bfloat16)

    def proj(w):
        return silu(jnp.dot(normed, w[...], preferred_element_type=jnp.float32)).astype(jnp.bfloat16)

    gate_out[...] = proj(wu)
    v = proj(wv).astype(jnp.float32)
    k = proj(wk).astype(jnp.float32)
    qk = q[...].astype(jnp.float32) * k
    for j in range(2):
        cols = slice(j * HEAD, (j + 1) * HEAD)
        s = jnp.sum(qk[:, cols], axis=1, keepdims=True) * SCALE + self_bias[i * 2 + j]
        self_out[:, cols] = silu(s) * v[:, cols]


def rest(tokens, w, q, self_bias):
    return pl.pallas_call(
        rest_kernel,
        grid=(4,),
        out_shape=(
            jax.ShapeDtypeStruct((ROWS, D), jnp.bfloat16),
            jax.ShapeDtypeStruct((ROWS, D), jnp.float32),
        ),
        in_specs=[
            pl.BlockSpec((ROWS, D), lambda i: (0, 0)),
            pl.BlockSpec((D, 256), lambda i: (0, i)),
            pl.BlockSpec((D, 256), lambda i: (0, 4 + i)),
            pl.BlockSpec((D, 256), lambda i: (0, 12 + i)),
            pl.BlockSpec((ROWS, 256), lambda i: (0, i)),
            SM,
        ],
        out_specs=(
            pl.BlockSpec((ROWS, 256), lambda i: (0, i)),
            pl.BlockSpec((ROWS, 256), lambda i: (0, i)),
        ),
        compiler_params=params(24),
        name="project_rest",
    )(tokens, w, w, w, q, self_bias)


def attend_kernel(tab, where, bias, q, kv, own, other, acc):
    z, core, h = where[0], where[1], where[2]
    o = z * 2 + core

    def one(d, out, s):
        acc[...] = jnp.zeros_like(acc)
        for c in range(CAP):
            slot = tab[d, o * CAP + c]

            @pl.when(slot >= 0)
            def _():
                p = tab[d, NG * CAP + o * CAP + c]
                limit = tab[d, 2 * NG * CAP] - p * BLOCK
                b = bias[h, p] * 0.5
                k = kv[:, 0, slot].reshape(BLOCK, HEAD)
                v = kv[:, 1, slot].reshape(BLOCK, HEAD)
                token = lax.broadcasted_iota(jnp.int32, (BLOCK, HEAD), 0)
                v = jnp.where(token < limit, v, jnp.zeros_like(v))
                for r in range(4):
                    rows = pl.ds(r * 128, 128)
                    scores = lax.dot_general(
                        q[d, rows], k, (((1,), (1,)), ((), ())), preferred_element_type=jnp.float32
                    )
                    t = scores * (0.5 * SCALE) + b
                    w = (t + t * jnp.tanh(t)).astype(jnp.bfloat16)
                    acc[rows] += jnp.dot(w, v, preferred_element_type=jnp.float32)

        out[s] = acc[...].astype(jnp.bfloat16)

    def step(s, carry):
        zz = lax.rem(z + s, NZ)
        one(zz * 2 + 1 - core, other, s)
        one(zz * 2 + core, own, s)
        return carry

    lax.fori_loop(0, NZ, step, 0)


def attend(tab, where, bias, q, kv):
    shape = jax.ShapeDtypeStruct((NZ, HALF, HEAD), jnp.bfloat16)
    return pl.pallas_call(
        attend_kernel,
        out_shape=(shape, shape),
        in_specs=[SM, SM, SM, VM, VM],
        out_specs=(VM, VM),
        scratch_shapes=[pltpu.VMEM((HALF, HEAD), jnp.float32)],
        compiler_params=params(32),
        name="attend",
    )(tab, where, bias, q, kv)


def pair_kernel(a, b, *outs):
    for s in range(NZ):
        outs[s][...] = (a[s].astype(jnp.float32) + b[s].astype(jnp.float32)).astype(jnp.bfloat16)


def pair(a, b):
    return pl.pallas_call(
        pair_kernel,
        out_shape=[jax.ShapeDtypeStruct((HALF, HEAD), jnp.bfloat16)] * NZ,
        in_specs=[VM, VM],
        out_specs=[VM] * NZ,
        compiler_params=params(16),
        name="add_pair",
    )(a, b)


def total_kernel(*refs):
    out = refs[-1]
    total = refs[0][...].astype(jnp.float32)
    for r in refs[1:-1]:
        total += r[...].astype(jnp.float32)
    out[...] = total.astype(jnp.bfloat16).reshape(NM, 32, HEAD)


def total(parts):
    return pl.pallas_call(
        total_kernel,
        out_shape=jax.ShapeDtypeStruct((NM, 32, HEAD), jnp.bfloat16),
        in_specs=[VM] * len(parts),
        out_specs=VM,
        compiler_params=params(16),
        name="add_groups",
    )(*parts)


def tail_kernel(hist, self_term, gate, tokens, w, where, count, out):
    cols = []
    for h in range(HEADS):
        cols.append(jnp.concatenate([hist[h * 2], hist[h * 2 + 1]], axis=0))
    attended = jnp.concatenate(cols, axis=1).astype(jnp.float32) + self_term[...]
    gated = (norm(attended) * gate[...].astype(jnp.float32)).astype(jnp.bfloat16)
    res = jnp.dot(gated, w[...], preferred_element_type=jnp.float32) + tokens[...].astype(jnp.float32)
    row = where[3] * ROWS + lax.broadcasted_iota(jnp.int32, (ROWS, D), 0)
    out[...] = jnp.where(row < count[0], res, 0.0).astype(jnp.bfloat16)


def tail(hist, self_term, gate, tokens, w, where, count):
    return pl.pallas_call(
        tail_kernel,
        out_shape=jax.ShapeDtypeStruct((ROWS, D), jnp.bfloat16),
        in_specs=[VM, VM, VM, VM, VM, SM, SM],
        out_specs=VM,
        compiler_params=params(16),
        name="output",
    )(hist, self_term, gate, tokens, w, where, count)


def local(
    tokens,
    in_weight,
    out_weight,
    history_pool,
    position_bias,
    self_bias,
    history_length,
    candidate_count,
    block_slots,
    block_position,
):
    z, core, m = lax.axis_index("z"), lax.axis_index("core"), lax.axis_index(M)
    where = jnp.stack([z, core, m // 2, m]).astype(jnp.int32)
    mine = jnp.concatenate(
        [
            block_slots.reshape(1, NG * CAP),
            block_position.reshape(1, NG * CAP),
            jnp.broadcast_to(history_length[:, None], (1, 64)),
        ],
        axis=1,
    )
    tab = lax.all_gather(mine, G, axis=0, tiled=True)
    packed = pack(history_pool)
    kv = lax.all_to_all(packed, M, split_axis=0, concat_axis=0, tiled=True)
    q, q_send = query(tokens, in_weight)
    q_mine = lax.all_to_all(q_send, M, split_axis=0, concat_axis=0, tiled=True)
    q_all = lax.all_gather(q_mine.reshape(1, HALF, HEAD), G, axis=0, tiled=True)
    gate, self_term = rest(tokens, in_weight, q, self_bias)
    own, other = attend(tab, where, position_bias, q_all, kv)
    other = lax.ppermute(other, "core", [(0, 1), (1, 0)])
    sums = pair(own, other)
    parts = [sums[0]]
    for s in range(1, NZ):
        parts.append(lax.ppermute(sums[s], "z", [(i, (i + s) % NZ) for i in range(NZ)]))
    hist = lax.all_to_all(total(parts), M, split_axis=0, concat_axis=0, tiled=True)
    return tail(hist, self_term, gate, tokens, out_weight, where, candidate_count)


def solution(mesh):
    fine = Mesh(mesh.devices.reshape(NZ, 2, 4, 4), ("z", "core", "x", "y"))
    placed = (
        P(("z", "core", "x", "y"), None),
        P(),
        P(),
        P(("z", "core"), ("x", "y"), None),
        P(),
        P(),
        P(("z", "core")),
        P(("z", "core")),
        P(("z", "core"), None, None),
        P(("z", "core"), None, None),
    )
    return jax.shard_map(
        local, mesh=fine, in_specs=placed, out_specs=P(("z", "core", "x", "y"), None), check_vma=False
    )
```

```python
import functools

import jax
import jax.numpy as jnp
from jax import lax
from jax.experimental import pallas as pl
from jax.experimental.pallas import tpu as pltpu
from jax.sharding import Mesh, PartitionSpec as P

D = 1024
HEADS = 8
HEAD = 128
BLOCK = 512
BLK = 14
CAP = 2
NZ = 8
NG = 16
NM = 16
SLAB = 32
ROWS = 64
HALF = 512
QROWS = 528
CUT = 256
EPS = 1e-05
SCALE = HEAD**-0.5
G = ("z", "core")
M = ("x", "y")
VM = pl.BlockSpec(memory_space=pltpu.VMEM)
SM = pl.BlockSpec(memory_space=pltpu.SMEM)
HB = pl.BlockSpec(memory_space=pltpu.HBM)


def params(mib):
    return pltpu.CompilerParams(vmem_limit_bytes=mib << 20)


def norm(values):
    center = values - jnp.mean(values, axis=-1, keepdims=True)
    spread = jnp.mean(center * center, axis=-1, keepdims=True)
    return center * lax.rsqrt(spread + EPS)


def silu(v):
    t = 0.5 * v
    return t + t * jnp.tanh(t)


def pack_kernel(pool, after, out):
    for h in range(HEADS):
        for kv in range(2):
            cols = pool[:, :, kv * D + h * HEAD : kv * D + (h + 1) * HEAD]
            for ch in range(2):
                out[h * 2 + ch, kv] = cols


def pack(pool, after):
    return pl.pallas_call(
        pack_kernel,
        out_shape=jax.ShapeDtypeStruct((NM, 2, BLK, SLAB, HEAD), jnp.bfloat16),
        in_specs=[VM, VM],
        out_specs=VM,
        compiler_params=params(16),
        name="pack_history",
    )(pool, after)


def query_kernel(tokens, w, q_out, send_out, buf, sems):
    copies = [
        pltpu.make_async_copy(w.at[:, pl.ds(2 * D + i * 256, 256)], buf.at[i], sems.at[i]) for i in range(4)
    ]
    for c in copies:
        c.start()
    normed = norm(tokens[...].astype(jnp.float32)).astype(jnp.bfloat16)
    for i in range(4):
        copies[i].wait()
        q = silu(jnp.dot(normed, buf[i], preferred_element_type=jnp.float32)).astype(jnp.bfloat16)
        q_out[:, i * 256 : (i + 1) * 256] = q
        for j in range(2):
            for ch in range(2):
                send_out[i * 4 + j * 2 + ch] = q[ch * 32 : ch * 32 + 32, j * HEAD : (j + 1) * HEAD]


def query(tokens, w):
    return pl.pallas_call(
        query_kernel,
        out_shape=(
            jax.ShapeDtypeStruct((ROWS, D), jnp.bfloat16),
            jax.ShapeDtypeStruct((NM, 32, HEAD), jnp.bfloat16),
        ),
        in_specs=[VM, HB],
        out_specs=(VM, VM),
        scratch_shapes=[pltpu.VMEM((4, D, 256), jnp.bfloat16), pltpu.SemaphoreType.DMA((4,))],
        compiler_params=params(16),
        name="project_query",
    )(tokens, pltpu.with_memory_space_constraint(w, pltpu.HBM))


def rest_kernel(tokens, w, q, self_bias, w2, gate_out, self_out, w2_out, buf, sems, sem):
    held = pltpu.make_async_copy(w2, w2_out, sem)
    held.start()
    copies = []
    for i in range(4):
        for j, base in enumerate((0, D, 3 * D)):
            n = i * 3 + j
            copies.append(
                pltpu.make_async_copy(w.at[:, pl.ds(base + i * 256, 256)], buf.at[n], sems.at[n])
            )
    for c in copies:
        c.start()
    normed = norm(tokens[...].astype(jnp.float32)).astype(jnp.bfloat16)

    def proj(n):
        copies[n].wait()
        return silu(jnp.dot(normed, buf[n], preferred_element_type=jnp.float32)).astype(jnp.bfloat16)

    for i in range(4):
        wide = slice(i * 256, (i + 1) * 256)
        gate_out[:, wide] = proj(i * 3)
        v = proj(i * 3 + 1).astype(jnp.float32)
        k = proj(i * 3 + 2).astype(jnp.float32)
        qk = q[:, wide].astype(jnp.float32) * k
        for j in range(2):
            cols = slice(j * HEAD, (j + 1) * HEAD)
            s = jnp.sum(qk[:, cols], axis=1, keepdims=True) * SCALE + self_bias[i * 2 + j]
            self_out[:, i * 256 + j * HEAD : i * 256 + (j + 1) * HEAD] = silu(s) * v[:, cols]
    held.wait()


def rest(tokens, w, q, self_bias, w2):
    return pl.pallas_call(
        rest_kernel,
        out_shape=(
            jax.ShapeDtypeStruct((ROWS, D), jnp.bfloat16),
            jax.ShapeDtypeStruct((ROWS, D), jnp.float32),
            pltpu.VMEM((D, D), jnp.bfloat16),
        ),
        in_specs=[VM, HB, VM, SM, HB],
        out_specs=(VM, VM, VM),
        scratch_shapes=[
            pltpu.VMEM((12, D, 256), jnp.bfloat16),
            pltpu.SemaphoreType.DMA((12,)),
            pltpu.SemaphoreType.DMA,
        ],
        compiler_params=params(20),
        name="project_rest",
    )(
        tokens,
        pltpu.with_memory_space_constraint(w, pltpu.HBM),
        q,
        self_bias,
        pltpu.with_memory_space_constraint(w2, pltpu.HBM),
    )


def stack_kernel(own, p1, m1, p2, m2, p3, m3, p4, m4, out):
    for s, piece in ((0, own), (7, p1), (1, m1), (6, p2), (2, m2), (5, p3), (3, m3)):
        out[s] = piece[...]
    out[4, :CUT] = p4[...]
    out[4, CUT:] = m4[...]


def stack(pieces):
    return pl.pallas_call(
        stack_kernel,
        out_shape=jax.ShapeDtypeStruct((NZ, QROWS, HEAD), jnp.bfloat16),
        in_specs=[VM] * 9,
        out_specs=VM,
        compiler_params=params(16),
        name="stack_queries",
    )(*pieces)


def table_kernel(q_own, q_other, tab, ints, sem):
    for i, q in enumerate((q_own, q_other)):
        for s in range(NZ):
            ints[i * NZ + s] = q[s, HALF:].astype(jnp.float32).astype(jnp.int32)[0:8]
    copy = pltpu.make_async_copy(ints.at[:, 0], tab, sem)
    copy.start()
    copy.wait()


def table(q_own, q_other):
    return pl.pallas_call(
        table_kernel,
        out_shape=jax.ShapeDtypeStruct((NG, 128), jnp.int32),
        in_specs=[VM, VM],
        out_specs=SM,
        scratch_shapes=[pltpu.VMEM((NG, 8, 128), jnp.int32), pltpu.SemaphoreType.DMA],
        compiler_params=params(16),
        name="read_tables",
    )(q_own, q_other)


def attend_kernel(first, count, base, tab, where, bias, q, kv, out, weights):
    h = where[2]
    o = where[0] * 2 + where[1]

    def weigh(i, carry):
        s = where[8 + first + i]
        row = base + s
        length = tab[row, 2 * NG * CAP] * 256 + tab[row, 2 * NG * CAP + 1]
        for c in range(CAP):
            slot = tab[row, o * CAP + c]

            @pl.when(slot >= 0)
            def _():
                p = tab[row, NG * CAP + o * CAP + c]
                b = bias[h, p] * 0.5
                keys = kv[:, 0, slot].reshape(BLOCK, HEAD)
                for j in range(4):
                    rows = pl.ds(j * 128, 128)
                    scores = lax.dot_general(
                        q[s, rows], keys, (((1,), (1,)), ((), ())), preferred_element_type=jnp.float32
                    )
                    t = scores * (0.5 * SCALE) + b
                    weights[slot, rows] = (t + t * jnp.tanh(t)).astype(jnp.bfloat16)
                limit = length - p * BLOCK

                @pl.when(limit < BLOCK)
                def _():
                    token = lax.broadcasted_iota(jnp.int32, (128, BLOCK), 1)
                    for j in range(4):
                        rows = pl.ds(j * 128, 128)
                        w = weights[slot, rows].astype(jnp.float32)
                        weights[slot, rows] = jnp.where(token < limit, w, 0.0).astype(jnp.bfloat16)

        return carry

    def blend(i, carry):
        row = base + where[8 + first + i]
        one, two = tab[row, o * CAP], tab[row, o * CAP + 1]

        def store(slots):
            values = [kv[:, 1, n].reshape(BLOCK, HEAD) for n in slots]
            for j in range(4):
                rows = pl.ds(j * 128, 128)
                total = jnp.zeros((128, HEAD), jnp.float32)
                for n, v in zip(slots, values):
                    total += jnp.dot(weights[n, rows], v, preferred_element_type=jnp.float32)
                out[i, rows] = total.astype(jnp.bfloat16)

        @pl.when((one >= 0) & (two >= 0))
        def _():
            store((one, two))

        @pl.when((one >= 0) & (two < 0))
        def _():
            store((one,))

        @pl.when((one < 0) & (two >= 0))
        def _():
            store((two,))

        @pl.when((one < 0) & (two < 0))
        def _():
            store(())

        return carry

    lax.fori_loop(0, count, weigh, 0)
    lax.fori_loop(0, count, blend, 0)


def attend(first, count, base, tab, where, bias, q, kv):
    return pl.pallas_call(
        functools.partial(attend_kernel, first, count, base),
        out_shape=jax.ShapeDtypeStruct((count, HALF, HEAD), jnp.bfloat16),
        in_specs=[SM, SM, SM, VM, VM],
        out_specs=VM,
        scratch_shapes=[pltpu.VMEM((BLK, HALF, BLOCK), jnp.bfloat16)],
        compiler_params=params(20),
        name=f"attend_{first}_{base}",
    )(tab, where, bias, q, kv)


def add(*refs):
    total = refs[0].astype(jnp.float32)
    for r in refs[1:]:
        total += r.astype(jnp.float32)
    return total


def far_kernel(a, b, up, down, up4, down4):
    for out, slots in ((up, (0, 1)), (down, (4, 3))):
        for i, n in enumerate(slots):
            out[i] = add(a[n], b[n]).astype(jnp.bfloat16)
    four = add(a[2], b[2]).astype(jnp.bfloat16)
    up4[...] = four[:256]
    down4[...] = four[256:]


def far(a, b):
    two = jax.ShapeDtypeStruct((2, HALF, HEAD), jnp.bfloat16)
    half = jax.ShapeDtypeStruct((256, HEAD), jnp.bfloat16)
    return pl.pallas_call(
        far_kernel,
        out_shape=(two, two, half, half),
        in_specs=[VM] * 2,
        out_specs=(VM,) * 4,
        compiler_params=params(16),
        name="add_far",
    )(a, b)


def near_kernel(a, b, up, down, up4, down4, here, next_up, next_down):
    here[...] = add(a[0], b[0], up[0], down[0])
    top, low = slice(0, 256), slice(256, 512)
    next_up[top] = add(a[1, top], b[1, top], up[1, top], up4[...]).astype(jnp.bfloat16)
    next_up[low] = add(a[1, low], b[1, low], up[1, low]).astype(jnp.bfloat16)
    next_down[top] = add(a[2, top], b[2, top], down[1, top]).astype(jnp.bfloat16)
    next_down[low] = add(a[2, low], b[2, low], down[1, low], down4[...]).astype(jnp.bfloat16)


def near(*args):
    part = jax.ShapeDtypeStruct((HALF, HEAD), jnp.bfloat16)
    return pl.pallas_call(
        near_kernel,
        out_shape=(jax.ShapeDtypeStruct((HALF, HEAD), jnp.float32), part, part),
        in_specs=[VM] * 6,
        out_specs=(VM,) * 3,
        compiler_params=params(16),
        name="add_near",
    )(*args)


def total_kernel(here, up, down, out):
    out[...] = add(here[...], up[...], down[...]).astype(jnp.bfloat16).reshape(NM, 32, HEAD)


def total(*parts):
    return pl.pallas_call(
        total_kernel,
        out_shape=jax.ShapeDtypeStruct((NM, 32, HEAD), jnp.bfloat16),
        in_specs=[VM] * 3,
        out_specs=VM,
        compiler_params=params(16),
        name="add_groups",
    )(*parts)


def tail_kernel(hist, self_term, gate, tokens, w, where, count, out):
    cols = []
    for h in range(HEADS):
        cols.append(jnp.concatenate([hist[h * 2], hist[h * 2 + 1]], axis=0))
    attended = jnp.concatenate(cols, axis=1).astype(jnp.float32) + self_term[...]
    gated = (norm(attended) * gate[...].astype(jnp.float32)).astype(jnp.bfloat16)
    res = jnp.dot(gated, w[...], preferred_element_type=jnp.float32) + tokens[...].astype(jnp.float32)
    row = where[3] * ROWS + lax.broadcasted_iota(jnp.int32, (ROWS, D), 0)
    out[...] = jnp.where(row < count[0], res, 0.0).astype(jnp.bfloat16)


def tail(hist, self_term, gate, tokens, w, where, count):
    return pl.pallas_call(
        tail_kernel,
        out_shape=jax.ShapeDtypeStruct((ROWS, D), jnp.bfloat16),
        in_specs=[VM, VM, VM, VM, VM, SM, SM],
        out_specs=VM,
        compiler_params=params(16),
        name="output",
    )(hist, self_term, gate, tokens, w, where, count)


def move(value, step):
    return lax.ppermute(value, "z", [(i, (i + step) % NZ) for i in range(NZ)])


def swap(value):
    return lax.ppermute(value, "core", [(0, 1), (1, 0)])


def local(
    tokens,
    in_weight,
    out_weight,
    history_pool,
    position_bias,
    self_bias,
    history_length,
    candidate_count,
    block_slots,
    block_position,
):
    z, core, m = lax.axis_index("z"), lax.axis_index("core"), lax.axis_index(M)
    where = jnp.concatenate(
        [jnp.stack([z, core, m // 2, m, 0, 0, 0, 0]), jnp.array([1, 3, 4, 5, 7, 0, 2, 6])]
    ).astype(jnp.int32)
    length = history_length[:, None]
    mine = jnp.concatenate(
        [
            block_slots.reshape(1, NG * CAP),
            block_position.reshape(1, NG * CAP),
            length // 256,
            length % 256,
            jnp.zeros((1, 62), jnp.int32),
        ],
        axis=1,
    ).astype(jnp.bfloat16)
    mine = jnp.broadcast_to(mine, (16, 128))
    q, q_send = query(tokens, in_weight)
    q_mine = lax.all_to_all(q_send, M, split_axis=0, concat_axis=0, tiled=True)
    packed = pack(history_pool, q)
    q_mine, packed = lax.optimization_barrier((q_mine, packed))
    kv = lax.all_to_all(packed, M, split_axis=0, concat_axis=0, tiled=True)
    gate, self_term, w2 = rest(tokens, in_weight, q, self_bias, out_weight)
    q_mine = jnp.concatenate([q_mine.reshape(HALF, HEAD), mine], axis=0)
    q_mine, gate, self_term, w2 = lax.optimization_barrier((q_mine, gate, self_term, w2))
    p1, m1, p2, m2 = (move(q_mine, s) for s in (1, -1, 2, -2))
    p3, m3, p4, m4 = move(p2, 1), move(m2, -1), move(p2[:CUT], 2), move(m2[CUT:], -2)
    q_own = stack([q_mine, p1, m1, p2, m2, p3, m3, p4, m4])
    q_other = swap(q_own)
    tab = table(q_own, q_other)
    sums = []
    for first, count in ((0, 5), (5, 3)):
        other = swap(attend(first, count, NZ, tab, where, position_bias, q_other, kv))
        own = attend(first, count, 0, tab, where, position_bias, q_own, kv)
        sums.append((own, other))
    up, down, up4, down4 = far(*sums[0])
    up, down, up4, down4 = move(up, 1), move(down, -1), move(up4, 2), move(down4, -2)
    here, up, down = near(*sums[1], up, down, up4, down4)
    hist = lax.all_to_all(total(here, move(up, 2), move(down, -2)), M, split_axis=0, concat_axis=0, tiled=True)
    return tail(hist, self_term, gate, tokens, w2, where, candidate_count)


def solution(mesh):
    fine = Mesh(mesh.devices.reshape(NZ, 2, 4, 4), ("z", "core", "x", "y"))
    placed = (
        P(("z", "core", "x", "y"), None),
        P(),
        P(),
        P(("z", "core"), ("x", "y"), None),
        P(),
        P(),
        P(("z", "core")),
        P(("z", "core")),
        P(("z", "core"), None, None),
        P(("z", "core"), None, None),
    )
    return jax.shard_map(
        local, mesh=fine, in_specs=placed, out_specs=P(("z", "core", "x", "y"), None), check_vma=False
    )
```

```python
import functools

import jax
import jax.numpy as jnp
from jax import lax
from jax.experimental import pallas as pl
from jax.experimental.pallas import tpu as pltpu
from jax.sharding import Mesh, PartitionSpec as P

D = 1024
HEADS = 8
HEAD = 128
BLOCK = 512
BLK = 14
CAP = 2
NZ = 8
NG = 16
NM = 16
SLAB = 32
ROWS = 64
HALF = 512
QROWS = 528
CUT = 256
EPS = 1e-05
SCALE = HEAD**-0.5
G = ("z", "core")
M = ("x", "y")
VM = pl.BlockSpec(memory_space=pltpu.VMEM)
SM = pl.BlockSpec(memory_space=pltpu.SMEM)
HB = pl.BlockSpec(memory_space=pltpu.HBM)


def params(mib):
    return pltpu.CompilerParams(vmem_limit_bytes=mib << 20)


def norm(values):
    center = values - jnp.mean(values, axis=-1, keepdims=True)
    spread = jnp.mean(center * center, axis=-1, keepdims=True)
    return center * lax.rsqrt(spread + EPS)


def silu(v):
    t = 0.5 * v
    return t + t * jnp.tanh(t)


def pack_kernel(pool, after, out):
    for h in range(HEADS):
        for kv in range(2):
            cols = pool[:, :, kv * D + h * HEAD : kv * D + (h + 1) * HEAD]
            for ch in range(2):
                out[h * 2 + ch, kv] = cols


def pack(pool, after):
    return pl.pallas_call(
        pack_kernel,
        out_shape=jax.ShapeDtypeStruct((NM, 2, BLK, SLAB, HEAD), jnp.bfloat16),
        in_specs=[VM, VM],
        out_specs=VM,
        compiler_params=params(12),
        name="pack_history",
    )(pool, after)


def query_kernel(tokens, w, q_out, send_out, rows, buf, sems):
    first = pltpu.make_async_copy(tokens, rows, sems.at[4])
    first.start()
    copies = [
        pltpu.make_async_copy(w.at[:, pl.ds(2 * D + i * 256, 256)], buf.at[i], sems.at[i]) for i in range(4)
    ]
    for c in copies:
        c.start()
    first.wait()
    normed = norm(rows[...].astype(jnp.float32)).astype(jnp.bfloat16)
    for i in range(4):
        copies[i].wait()
        q = silu(jnp.dot(normed, buf[i], preferred_element_type=jnp.float32)).astype(jnp.bfloat16)
        q_out[:, i * 256 : (i + 1) * 256] = q
        for j in range(2):
            for ch in range(2):
                send_out[i * 4 + j * 2 + ch] = q[ch * 32 : ch * 32 + 32, j * HEAD : (j + 1) * HEAD]


def query(tokens, w):
    return pl.pallas_call(
        query_kernel,
        out_shape=(
            jax.ShapeDtypeStruct((ROWS, D), jnp.bfloat16),
            jax.ShapeDtypeStruct((NM, 32, HEAD), jnp.bfloat16),
        ),
        in_specs=[HB, HB],
        out_specs=(VM, VM),
        scratch_shapes=[
            pltpu.VMEM((ROWS, D), jnp.bfloat16),
            pltpu.VMEM((4, D, 256), jnp.bfloat16),
            pltpu.SemaphoreType.DMA((5,)),
        ],
        compiler_params=params(12),
        name="project_query",
    )(pltpu.with_memory_space_constraint(tokens, pltpu.HBM), pltpu.with_memory_space_constraint(w, pltpu.HBM))


def rest_kernel(tokens, w, q, self_bias, w2, gate_out, self_out, w2_out, buf, sems, sem):
    held = pltpu.make_async_copy(w2, w2_out, sem)
    held.start()
    copies = []
    for i in range(4):
        for j, base in enumerate((0, D, 3 * D)):
            n = i * 3 + j
            copies.append(
                pltpu.make_async_copy(w.at[:, pl.ds(base + i * 256, 256)], buf.at[n], sems.at[n])
            )
    for c in copies:
        c.start()
    normed = norm(tokens[...].astype(jnp.float32)).astype(jnp.bfloat16)

    def proj(n):
        copies[n].wait()
        return silu(jnp.dot(normed, buf[n], preferred_element_type=jnp.float32)).astype(jnp.bfloat16)

    for i in range(4):
        wide = slice(i * 256, (i + 1) * 256)
        gate_out[:, wide] = proj(i * 3)
        v = proj(i * 3 + 1).astype(jnp.float32)
        k = proj(i * 3 + 2).astype(jnp.float32)
        qk = q[:, wide].astype(jnp.float32) * k
        for j in range(2):
            cols = slice(j * HEAD, (j + 1) * HEAD)
            s = jnp.sum(qk[:, cols], axis=1, keepdims=True) * SCALE + self_bias[i * 2 + j]
            self_out[:, i * 256 + j * HEAD : i * 256 + (j + 1) * HEAD] = silu(s) * v[:, cols]
    held.wait()


def rest(tokens, w, q, self_bias, w2):
    return pl.pallas_call(
        rest_kernel,
        out_shape=(
            jax.ShapeDtypeStruct((ROWS, D), jnp.bfloat16),
            jax.ShapeDtypeStruct((ROWS, D), jnp.float32),
            pltpu.VMEM((D, D), jnp.bfloat16),
        ),
        in_specs=[VM, HB, VM, SM, HB],
        out_specs=(VM, VM, VM),
        scratch_shapes=[
            pltpu.VMEM((12, D, 256), jnp.bfloat16),
            pltpu.SemaphoreType.DMA((12,)),
            pltpu.SemaphoreType.DMA,
        ],
        compiler_params=params(20),
        name="project_rest",
    )(
        tokens,
        pltpu.with_memory_space_constraint(w, pltpu.HBM),
        q,
        self_bias,
        pltpu.with_memory_space_constraint(w2, pltpu.HBM),
    )


def bundle_kernel(own, low, high, up, down):
    up[:QROWS] = own[...]
    up[QROWS : 2 * QROWS] = high[...]
    up[2 * QROWS :] = low[:CUT]
    down[:QROWS] = own[...]
    down[QROWS : 2 * QROWS] = low[...]
    down[2 * QROWS :] = high[CUT:]


def bundle(own, low, high):
    return pl.pallas_call(
        bundle_kernel,
        out_shape=(
            jax.ShapeDtypeStruct((2 * QROWS + CUT, HEAD), jnp.bfloat16),
            jax.ShapeDtypeStruct((3 * QROWS - CUT, HEAD), jnp.bfloat16),
        ),
        in_specs=[VM] * 3,
        out_specs=(VM, VM),
        compiler_params=params(12),
        name="bundle_queries",
    )(own, low, high)


def stack_kernel(own, low, high, up, down, out):
    out[0] = own[...]
    out[5] = low[...]
    out[3] = high[...]
    out[7] = up[:QROWS]
    out[2] = up[QROWS : 2 * QROWS]
    out[4, :CUT] = up[2 * QROWS :]
    out[1] = down[:QROWS]
    out[6] = down[QROWS : 2 * QROWS]
    out[4, CUT:] = down[2 * QROWS :]


def stack(*pieces):
    return pl.pallas_call(
        stack_kernel,
        out_shape=jax.ShapeDtypeStruct((NZ, QROWS, HEAD), jnp.bfloat16),
        in_specs=[VM] * 5,
        out_specs=VM,
        compiler_params=params(12),
        name="stack_queries",
    )(*pieces)


def table_kernel(where, q_own, q_other, plan, tab, ints, sem):
    o = where[0] * 2 + where[1]
    for i, q in enumerate((q_own, q_other)):
        for s in range(NZ):
            ints[i * NZ + s] = q[s, HALF:].astype(jnp.float32).astype(jnp.int32)[0:8]
    copy = pltpu.make_async_copy(ints.at[:, 0], tab, sem)
    copy.start()
    for i in range(3):
        for b in range(16):
            plan[i, b] = -1
    copy.wait()

    def step(row, carry):
        length = tab[row, 2 * NG * CAP] * 256 + tab[row, 2 * NG * CAP + 1]
        for c in range(CAP):
            slot = tab[row, o * CAP + c]

            @pl.when(slot >= 0)
            def _():
                p = tab[row, NG * CAP + o * CAP + c]
                plan[0, slot] = row
                plan[1, slot] = p
                plan[2, slot] = length - p * BLOCK

        return carry

    lax.fori_loop(0, NG, step, 0)


def table(where, q_own, q_other):
    return pl.pallas_call(
        table_kernel,
        out_shape=jax.ShapeDtypeStruct((3, 16), jnp.int32),
        in_specs=[SM, VM, VM],
        out_specs=SM,
        scratch_shapes=[
            pltpu.SMEM((NG, 128), jnp.int32),
            pltpu.VMEM((NG, 8, 128), jnp.int32),
            pltpu.SemaphoreType.DMA,
        ],
        compiler_params=params(12),
        name="read_tables",
    )(where, q_own, q_other)


def attend_blocks(base, plan, where, bias, q, blocks, ready, out, acc):
    h = where[2]
    acc[...] = jnp.zeros_like(acc)
    for b in range(BLK):
        ready(b)
        row = plan[0, b]

        @pl.when((row >= base) & (row < base + NZ))
        def _():
            keys = blocks[b, :, 0].reshape(BLOCK, HEAD)
            values = blocks[b, :, 1].reshape(BLOCK, HEAD)
            token = lax.broadcasted_iota(jnp.int32, (BLOCK, HEAD), 0)
            values = jnp.where(token < plan[2, b], values, jnp.zeros_like(values))
            scores = lax.dot_general(
                q[row - base, :HALF], keys, (((1,), (1,)), ((), ())), preferred_element_type=jnp.float32
            )
            t = scores * (0.5 * SCALE) + bias[h, plan[1, b]] * 0.5
            weights = (t + t * jnp.tanh(t)).astype(jnp.bfloat16)
            acc[row - base] += jnp.dot(weights, values, preferred_element_type=jnp.float32)

    out[...] = acc[...].astype(jnp.bfloat16)


def other_kernel(plan, where, bias, q, kv, out, blocks, acc, sems):
    copies = [pltpu.make_async_copy(kv.at[:, :, b], blocks.at[b], sems.at[b]) for b in range(BLK)]
    for c in copies:
        c.start()
    attend_blocks(NZ, plan, where, bias, q, blocks, lambda b: copies[b].wait(), out, acc)


def own_kernel(plan, where, bias, q, blocks, out, acc):
    attend_blocks(0, plan, where, bias, q, blocks, lambda b: None, out, acc)


def attend_other(plan, where, bias, q, kv):
    return pl.pallas_call(
        other_kernel,
        out_shape=(
            jax.ShapeDtypeStruct((NZ, HALF, HEAD), jnp.bfloat16),
            jax.ShapeDtypeStruct((BLK, NM, 2, SLAB, HEAD), jnp.bfloat16),
        ),
        in_specs=[SM, SM, SM, VM, HB],
        out_specs=(VM, VM),
        scratch_shapes=[pltpu.VMEM((NZ, HALF, HEAD), jnp.float32), pltpu.SemaphoreType.DMA((BLK,))],
        compiler_params=params(16),
        name="attend_other",
    )(plan, where, bias, q, pltpu.with_memory_space_constraint(kv, pltpu.HBM))


def attend_own(plan, where, bias, q, blocks):
    return pl.pallas_call(
        own_kernel,
        out_shape=jax.ShapeDtypeStruct((NZ, HALF, HEAD), jnp.bfloat16),
        in_specs=[SM, SM, SM, VM, VM],
        out_specs=VM,
        scratch_shapes=[pltpu.VMEM((NZ, HALF, HEAD), jnp.float32)],
        compiler_params=params(16),
        name="attend_own",
    )(plan, where, bias, q, blocks)


def add(*refs):
    total = refs[0].astype(jnp.float32)
    for r in refs[1:]:
        total += r.astype(jnp.float32)
    return total


def far_kernel(a, b, up, down, across):
    for out, slots in ((up, (1, 3)), (down, (7, 5))):
        for i, s in enumerate(slots):
            out[i] = add(a[s], b[s]).astype(jnp.bfloat16)
    across[...] = add(a[4], b[4]).astype(jnp.bfloat16)


def far(a, b):
    two = jax.ShapeDtypeStruct((2, HALF, HEAD), jnp.bfloat16)
    return pl.pallas_call(
        far_kernel,
        out_shape=(two, two, jax.ShapeDtypeStruct((HALF, HEAD), jnp.bfloat16)),
        in_specs=[VM] * 2,
        out_specs=(VM,) * 3,
        compiler_params=params(12),
        name="add_far",
    )(a, b)


def near_kernel(a, b, up, down, here, next_up, next_down):
    here[...] = add(a[0], b[0], up[0], down[0])
    next_up[...] = add(a[2], b[2], up[1]).astype(jnp.bfloat16)
    next_down[...] = add(a[6], b[6], down[1]).astype(jnp.bfloat16)


def near(*args):
    part = jax.ShapeDtypeStruct((HALF, HEAD), jnp.bfloat16)
    return pl.pallas_call(
        near_kernel,
        out_shape=(jax.ShapeDtypeStruct((HALF, HEAD), jnp.float32), part, part),
        in_specs=[VM] * 4,
        out_specs=(VM,) * 3,
        compiler_params=params(12),
        name="add_near",
    )(*args)


def total_kernel(here, across, up, down, out):
    out[...] = add(here[...], across[...], up[...], down[...]).astype(jnp.bfloat16).reshape(NM, 32, HEAD)


def total(*parts):
    return pl.pallas_call(
        total_kernel,
        out_shape=jax.ShapeDtypeStruct((NM, 32, HEAD), jnp.bfloat16),
        in_specs=[VM] * 4,
        out_specs=VM,
        compiler_params=params(12),
        name="add_groups",
    )(*parts)


def tail_kernel(hist, self_term, gate, tokens, w, where, count, out):
    cols = []
    for h in range(HEADS):
        cols.append(jnp.concatenate([hist[h * 2], hist[h * 2 + 1]], axis=0))
    attended = jnp.concatenate(cols, axis=1).astype(jnp.float32) + self_term[...]
    gated = (norm(attended) * gate[...].astype(jnp.float32)).astype(jnp.bfloat16)
    res = jnp.dot(gated, w[...], preferred_element_type=jnp.float32) + tokens[...].astype(jnp.float32)
    row = where[3] * ROWS + lax.broadcasted_iota(jnp.int32, (ROWS, D), 0)
    out[...] = jnp.where(row < count[0], res, 0.0).astype(jnp.bfloat16)


def tail(hist, self_term, gate, tokens, w, where, count):
    return pl.pallas_call(
        tail_kernel,
        out_shape=jax.ShapeDtypeStruct((ROWS, D), jnp.bfloat16),
        in_specs=[VM, VM, VM, VM, VM, SM, SM],
        out_specs=VM,
        compiler_params=params(16),
        name="output",
    )(hist, self_term, gate, tokens, w, where, count)


def move(value, step):
    return lax.ppermute(value, "z", [(i, (i + step) % NZ) for i in range(NZ)])


def swap(value):
    return lax.ppermute(value, "core", [(0, 1), (1, 0)])


def local(
    tokens,
    in_weight,
    out_weight,
    history_pool,
    position_bias,
    self_bias,
    history_length,
    candidate_count,
    block_slots,
    block_position,
):
    z, core, m = lax.axis_index("z"), lax.axis_index("core"), lax.axis_index(M)
    where = jnp.stack([z, core, m // 2, m]).astype(jnp.int32)
    length = history_length[:, None]
    mine = jnp.concatenate(
        [
            block_slots.reshape(1, NG * CAP),
            block_position.reshape(1, NG * CAP),
            length // 256,
            length % 256,
            jnp.zeros((1, 62), jnp.int32),
        ],
        axis=1,
    ).astype(jnp.bfloat16)
    mine = jnp.broadcast_to(mine, (16, 128))
    q, q_send = query(tokens, in_weight)
    q_mine = lax.all_to_all(q_send, M, split_axis=0, concat_axis=0, tiled=True)
    packed = pack(history_pool, q)
    q_mine, packed = lax.optimization_barrier((q_mine, packed))
    kv = lax.all_to_all(packed, M, split_axis=0, concat_axis=0, tiled=True)
    mine = jnp.concatenate([q_mine.reshape(HALF, HEAD), mine], axis=0)
    low, high = move(mine, 3), move(mine, -3)
    up, down = bundle(mine, low, high)
    q_own = stack(mine, low, high, move(up, 1), move(down, -1))
    q_other = swap(q_own)
    plan = table(where, q_own, q_other)
    gate, self_term, w2 = rest(tokens, in_weight, q, self_bias, out_weight)
    kv, gate, self_term, w2, plan = lax.optimization_barrier((kv, gate, self_term, w2, plan))
    other, blocks = attend_other(plan, where, position_bias, q_other, kv)
    other = swap(other)
    own = attend_own(plan, where, position_bias, q_own, blocks)
    up, down, across = far(own, other)
    across = move(across, 4)
    here, up, down = near(own, other, move(up, 1), move(down, -1))
    hist = total(here, across, move(up, 2), move(down, -2))
    hist = lax.all_to_all(hist, M, split_axis=0, concat_axis=0, tiled=True)
    return tail(hist, self_term, gate, tokens, w2, where, candidate_count)


def solution(mesh):
    fine = Mesh(mesh.devices.reshape(NZ, 2, 4, 4), ("z", "core", "x", "y"))
    placed = (
        P(("z", "core", "x", "y"), None),
        P(),
        P(),
        P(("z", "core"), ("x", "y"), None),
        P(),
        P(),
        P(("z", "core")),
        P(("z", "core")),
        P(("z", "core"), None, None),
        P(("z", "core"), None, None),
    )
    return jax.shard_map(
        local, mesh=fine, in_specs=placed, out_specs=P(("z", "core", "x", "y"), None), check_vma=False
    )
```

```python
import functools

import jax
import jax.numpy as jnp
from jax import lax
from jax.experimental import pallas as pl
from jax.experimental.pallas import tpu as pltpu
from jax.sharding import Mesh, PartitionSpec as P

D = 1024
HEADS = 8
HEAD = 128
BLOCK = 512
BLK = 14
CAP = 2
NZ = 8
NG = 16
NM = 16
SLAB = 32
ROWS = 64
HALF = 512
QROWS = 528
CUT = 272
FIRST = 9
EPS = 1e-05
SCALE = HEAD**-0.5
G = ("z", "core")
M = ("x", "y")
VM = pl.BlockSpec(memory_space=pltpu.VMEM)
SM = pl.BlockSpec(memory_space=pltpu.SMEM)
HB = pl.BlockSpec(memory_space=pltpu.HBM)


def params(mib):
    return pltpu.CompilerParams(vmem_limit_bytes=mib << 20)


def norm(values):
    center = values - jnp.mean(values, axis=-1, keepdims=True)
    spread = jnp.mean(center * center, axis=-1, keepdims=True)
    return center * lax.rsqrt(spread + EPS)


def silu(v):
    t = 0.5 * v
    return t + t * jnp.tanh(t)


def pack_kernel(pool, after, out):
    for h in range(HEADS):
        for kv in range(2):
            cols = pool[:, :, kv * D + h * HEAD : kv * D + (h + 1) * HEAD]
            for ch in range(2):
                out[h * 2 + ch, kv] = cols


def pack(pool, after):
    return pl.pallas_call(
        pack_kernel,
        out_shape=jax.ShapeDtypeStruct((NM, 2, BLK, SLAB, HEAD), jnp.bfloat16),
        in_specs=[VM, VM],
        out_specs=VM,
        compiler_params=params(12),
        name="pack_history",
    )(pool, after)


def query_kernel(tokens, w, q_out, send_out, rows, buf, sems):
    first = pltpu.make_async_copy(tokens, rows, sems.at[4])
    first.start()
    copies = [
        pltpu.make_async_copy(w.at[:, pl.ds(2 * D + i * 256, 256)], buf.at[i], sems.at[i]) for i in range(4)
    ]
    for c in copies:
        c.start()
    first.wait()
    normed = norm(rows[...].astype(jnp.float32)).astype(jnp.bfloat16)
    for i in range(4):
        copies[i].wait()
        q = silu(jnp.dot(normed, buf[i], preferred_element_type=jnp.float32)).astype(jnp.bfloat16)
        q_out[:, i * 256 : (i + 1) * 256] = q
        for j in range(2):
            for ch in range(2):
                send_out[i * 4 + j * 2 + ch] = q[ch * 32 : ch * 32 + 32, j * HEAD : (j + 1) * HEAD]


def query(tokens, w):
    return pl.pallas_call(
        query_kernel,
        out_shape=(
            jax.ShapeDtypeStruct((ROWS, D), jnp.bfloat16),
            jax.ShapeDtypeStruct((NM, 32, HEAD), jnp.bfloat16),
        ),
        in_specs=[HB, HB],
        out_specs=(VM, VM),
        scratch_shapes=[
            pltpu.VMEM((ROWS, D), jnp.bfloat16),
            pltpu.VMEM((4, D, 256), jnp.bfloat16),
            pltpu.SemaphoreType.DMA((5,)),
        ],
        compiler_params=params(12),
        name="project_query",
    )(pltpu.with_memory_space_constraint(tokens, pltpu.HBM), pltpu.with_memory_space_constraint(w, pltpu.HBM))


def rest_kernel(tokens, w, q, self_bias, w2, gate_out, self_out, w2_out, buf, sems, sem):
    held = pltpu.make_async_copy(w2, w2_out, sem)
    held.start()
    copies = []
    for i in range(4):
        for j, base in enumerate((0, D, 3 * D)):
            n = i * 3 + j
            copies.append(
                pltpu.make_async_copy(w.at[:, pl.ds(base + i * 256, 256)], buf.at[n], sems.at[n])
            )
    for c in copies:
        c.start()
    normed = norm(tokens[...].astype(jnp.float32)).astype(jnp.bfloat16)

    def proj(n):
        copies[n].wait()
        return silu(jnp.dot(normed, buf[n], preferred_element_type=jnp.float32)).astype(jnp.bfloat16)

    for i in range(4):
        wide = slice(i * 256, (i + 1) * 256)
        gate_out[:, wide] = proj(i * 3)
        v = proj(i * 3 + 1).astype(jnp.float32)
        k = proj(i * 3 + 2).astype(jnp.float32)
        qk = q[:, wide].astype(jnp.float32) * k
        for j in range(2):
            cols = slice(j * HEAD, (j + 1) * HEAD)
            s = jnp.sum(qk[:, cols], axis=1, keepdims=True) * SCALE + self_bias[i * 2 + j]
            self_out[:, i * 256 + j * HEAD : i * 256 + (j + 1) * HEAD] = silu(s) * v[:, cols]
    held.wait()


def rest(tokens, w, q, self_bias, w2):
    return pl.pallas_call(
        rest_kernel,
        out_shape=(
            jax.ShapeDtypeStruct((ROWS, D), jnp.bfloat16),
            jax.ShapeDtypeStruct((ROWS, D), jnp.float32),
            pltpu.VMEM((D, D), jnp.bfloat16),
        ),
        in_specs=[VM, HB, VM, SM, HB],
        out_specs=(VM, VM, VM),
        scratch_shapes=[
            pltpu.VMEM((12, D, 256), jnp.bfloat16),
            pltpu.SemaphoreType.DMA((12,)),
            pltpu.SemaphoreType.DMA,
        ],
        compiler_params=params(20),
        name="project_rest",
    )(
        tokens,
        pltpu.with_memory_space_constraint(w, pltpu.HBM),
        q,
        self_bias,
        pltpu.with_memory_space_constraint(w2, pltpu.HBM),
    )


def by_side(where, body, first, second, width=1):
    even = lax.rem(lax.div(where[0], width), 2) == 0

    @pl.when(even)
    def _():
        body(*first, *second)

    @pl.when(jnp.logical_not(even))
    def _():
        body(*second, *first)


def bundle_kernel(where, own, far_a, far_b, out_a, out_b):
    def body(high, up, low, down):
        up[:QROWS] = own[...]
        up[QROWS : 2 * QROWS] = high[...]
        up[2 * QROWS :] = low[:CUT]
        down[:QROWS] = own[...]
        down[QROWS : 2 * QROWS] = low[...]
        down[2 * QROWS :] = high[QROWS - CUT :]

    by_side(where, body, (far_a, out_a), (far_b, out_b))


def bundle(*args):
    shape = jax.ShapeDtypeStruct((2 * QROWS + CUT, HEAD), jnp.bfloat16)
    return pl.pallas_call(
        bundle_kernel,
        out_shape=(shape, shape),
        in_specs=[SM] + [VM] * 3,
        out_specs=(VM, VM),
        compiler_params=params(12),
        name="bundle_queries",
    )(*args)


def stack_kernel(where, own, far_a, far_b, near_a, near_b, out):
    def body(high, plus, low, minus):
        out[0] = own[...]
        out[5] = low[...]
        out[3] = high[...]
        out[7] = minus[:QROWS]
        out[2] = minus[QROWS : 2 * QROWS]
        out[4, :CUT] = minus[2 * QROWS :]
        out[1] = plus[:QROWS]
        out[6] = plus[QROWS : 2 * QROWS]
        out[4, QROWS - CUT :] = plus[2 * QROWS :]

    by_side(where, body, (far_a, near_a), (far_b, near_b))


def stack(*args):
    return pl.pallas_call(
        stack_kernel,
        out_shape=jax.ShapeDtypeStruct((NZ, QROWS, HEAD), jnp.bfloat16),
        in_specs=[SM] + [VM] * 5,
        out_specs=VM,
        compiler_params=params(12),
        name="stack_queries",
    )(*args)


def table_kernel(where, q_own, q_other, plan, tab, ints, sem):
    o = where[0] * 2 + where[1]
    for i, q in enumerate((q_own, q_other)):
        for s in range(NZ):
            ints[i * NZ + s] = q[s, HALF:].astype(jnp.float32).astype(jnp.int32)[0:8]
    copy = pltpu.make_async_copy(ints.at[:, 0], tab, sem)
    copy.start()
    for i in range(4):
        for b in range(16):
            plan[i, b] = -1
    copy.wait()

    def step(row, carry):
        length = tab[row, 2 * NG * CAP] * 256 + tab[row, 2 * NG * CAP + 1]
        for c in range(CAP):
            slot = tab[row, o * CAP + c]

            @pl.when(slot >= 0)
            def _():
                p = tab[row, NG * CAP + o * CAP + c]
                plan[0, slot] = row
                plan[1, slot] = p
                plan[2, slot] = length - p * BLOCK

        return carry

    lax.fori_loop(0, NG, step, 0)
    budget = FIRST
    for b in range(BLK):
        budget -= (plan[0, b] >= NZ).astype(jnp.int32)
    for b in range(BLK):
        row = plan[0, b]
        mine = (row >= 0) & (row < NZ)
        later = mine & (budget <= 0)
        budget -= mine.astype(jnp.int32)
        plan[3, b] = jnp.where(row < 0, -1, jnp.where(later, 1, 0))


def table(where, q_own, q_other):
    return pl.pallas_call(
        table_kernel,
        out_shape=jax.ShapeDtypeStruct((4, 16), jnp.int32),
        in_specs=[SM, VM, VM],
        out_specs=SM,
        scratch_shapes=[
            pltpu.SMEM((NG, 128), jnp.int32),
            pltpu.VMEM((NG, 8, 128), jnp.int32),
            pltpu.SemaphoreType.DMA,
        ],
        compiler_params=params(12),
        name="read_tables",
    )(where, q_own, q_other)


def attend_blocks(phase, plan, where, bias, pick, blocks, ready, acc):
    h = where[2]
    for b in range(BLK):
        ready(b)

        @pl.when(plan[3, b] == phase)
        def _():
            row = plan[0, b]
            keys = blocks[b, :, 0].reshape(BLOCK, HEAD)
            values = blocks[b, :, 1].reshape(BLOCK, HEAD)
            token = lax.broadcasted_iota(jnp.int32, (BLOCK, HEAD), 0)
            values = jnp.where(token < plan[2, b], values, jnp.zeros_like(values))
            scores = lax.dot_general(
                pick(row), keys, (((1,), (1,)), ((), ())), preferred_element_type=jnp.float32
            )
            t = scores * (0.5 * SCALE) + bias[h, plan[1, b]] * 0.5
            weights = (t + t * jnp.tanh(t)).astype(jnp.bfloat16)
            acc[row] += jnp.dot(weights, values, preferred_element_type=jnp.float32)


def first_kernel(plan, where, bias, q_own, q_other, kv, own, other, blocks, acc, sems):
    copies = [pltpu.make_async_copy(kv.at[:, :, b], blocks.at[b], sems.at[b]) for b in range(BLK)]
    for c in copies:
        c.start()
    acc[...] = jnp.zeros_like(acc)

    def pick(row):
        return jnp.where(row < NZ, q_own[lax.rem(row, NZ), :HALF], q_other[lax.rem(row, NZ), :HALF])

    attend_blocks(0, plan, where, bias, pick, blocks, lambda b: copies[b].wait(), acc)
    own[...] = acc[:NZ]
    other[...] = acc[NZ:].astype(jnp.bfloat16)


def second_kernel(plan, where, bias, q, blocks, own, out, acc):
    acc[...] = own[...]
    attend_blocks(1, plan, where, bias, lambda row: q[row, :HALF], blocks, lambda b: None, acc)
    out[...] = acc[...].astype(jnp.bfloat16)


def attend_first(plan, where, bias, q_own, q_other, kv):
    return pl.pallas_call(
        first_kernel,
        out_shape=(
            jax.ShapeDtypeStruct((NZ, HALF, HEAD), jnp.float32),
            jax.ShapeDtypeStruct((NZ, HALF, HEAD), jnp.bfloat16),
            jax.ShapeDtypeStruct((BLK, NM, 2, SLAB, HEAD), jnp.bfloat16),
        ),
        in_specs=[SM, SM, SM, VM, VM, HB],
        out_specs=(VM, VM, VM),
        scratch_shapes=[pltpu.VMEM((NG, HALF, HEAD), jnp.float32), pltpu.SemaphoreType.DMA((BLK,))],
        compiler_params=params(20),
        name="attend_first",
    )(plan, where, bias, q_own, q_other, pltpu.with_memory_space_constraint(kv, pltpu.HBM))


def attend_second(plan, where, bias, q, blocks, own):
    return pl.pallas_call(
        second_kernel,
        out_shape=jax.ShapeDtypeStruct((NZ, HALF, HEAD), jnp.bfloat16),
        in_specs=[SM, SM, SM, VM, VM, VM],
        out_specs=VM,
        scratch_shapes=[pltpu.VMEM((NZ, HALF, HEAD), jnp.float32)],
        compiler_params=params(16),
        name="attend_second",
    )(plan, where, bias, q, blocks, own)


def add(*refs):
    total = refs[0].astype(jnp.float32)
    for r in refs[1:]:
        total += r.astype(jnp.float32)
    return total


def far_kernel(where, a, b, out_a, out_b, half_a, half_b):
    def body(up, down):
        up[...] = add(a[3], b[3]).astype(jnp.bfloat16)
        down[...] = add(a[5], b[5]).astype(jnp.bfloat16)

    def opposite(up, down):
        up[...] = add(a[4, :256], b[4, :256]).astype(jnp.bfloat16)
        down[...] = add(a[4, 256:], b[4, 256:]).astype(jnp.bfloat16)

    by_side(where, body, (out_a,), (out_b,))
    by_side(where, opposite, (half_a,), (half_b,), 2)


def far(*args):
    part = jax.ShapeDtypeStruct((HALF, HEAD), jnp.bfloat16)
    half = jax.ShapeDtypeStruct((256, HEAD), jnp.bfloat16)
    return pl.pallas_call(
        far_kernel,
        out_shape=(part, part, half, half),
        in_specs=[SM] + [VM] * 2,
        out_specs=(VM,) * 4,
        compiler_params=params(12),
        name="add_far",
    )(*args)


def side_kernel(where, a, b, after, out_a, out_b):
    def body(up, down):
        up[...] = add(a[1], b[1]).astype(jnp.bfloat16)
        down[...] = add(a[7], b[7]).astype(jnp.bfloat16)

    by_side(where, body, (out_a,), (out_b,))


def side(*args):
    part = jax.ShapeDtypeStruct((HALF, HEAD), jnp.bfloat16)
    return pl.pallas_call(
        side_kernel,
        out_shape=(part, part),
        in_specs=[SM] + [VM] * 3,
        out_specs=(VM,) * 2,
        compiler_params=params(12),
        name="add_side",
    )(*args)


def near_kernel(where, a, b, near_a, near_b, half_a, half_b, out_a, out_b, ups, downs):
    def body(plus, minus):
        ups[...] = add(a[2], b[2], minus[...])
        downs[...] = add(a[6], b[6], plus[...])

    def opposite(plus, up, minus, down):
        up[:256] = add(ups[:256], minus[...]).astype(jnp.bfloat16)
        up[256:] = ups[256:].astype(jnp.bfloat16)
        down[:256] = downs[:256].astype(jnp.bfloat16)
        down[256:] = add(downs[256:], plus[...]).astype(jnp.bfloat16)

    by_side(where, body, (near_a,), (near_b,))
    by_side(where, opposite, (half_a, out_a), (half_b, out_b), 2)


def near(*args):
    part = jax.ShapeDtypeStruct((HALF, HEAD), jnp.bfloat16)
    return pl.pallas_call(
        near_kernel,
        out_shape=(part, part),
        in_specs=[SM] + [VM] * 6,
        out_specs=(VM,) * 2,
        scratch_shapes=[pltpu.VMEM((HALF, HEAD), jnp.float32)] * 2,
        compiler_params=params(12),
        name="add_near",
    )(*args)


def total_kernel(own, other, *refs):
    total = add(own[0], other[0], *(r[...] for r in refs[:-1]))
    refs[-1][...] = total.astype(jnp.bfloat16).reshape(NM, 32, HEAD)


def total(*parts):
    return pl.pallas_call(
        total_kernel,
        out_shape=jax.ShapeDtypeStruct((NM, 32, HEAD), jnp.bfloat16),
        in_specs=[VM] * 6,
        out_specs=VM,
        compiler_params=params(12),
        name="add_groups",
    )(*parts)


def tail_kernel(hist, self_term, gate, tokens, w, where, count, out):
    cols = []
    for h in range(HEADS):
        cols.append(jnp.concatenate([hist[h * 2], hist[h * 2 + 1]], axis=0))
    attended = jnp.concatenate(cols, axis=1).astype(jnp.float32) + self_term[...]
    gated = (norm(attended) * gate[...].astype(jnp.float32)).astype(jnp.bfloat16)
    res = jnp.dot(gated, w[...], preferred_element_type=jnp.float32) + tokens[...].astype(jnp.float32)
    row = where[3] * ROWS + lax.broadcasted_iota(jnp.int32, (ROWS, D), 0)
    out[...] = jnp.where(row < count[0], res, 0.0).astype(jnp.bfloat16)


def tail(hist, self_term, gate, tokens, w, where, count):
    return pl.pallas_call(
        tail_kernel,
        out_shape=jax.ShapeDtypeStruct((ROWS, D), jnp.bfloat16),
        in_specs=[VM, VM, VM, VM, VM, SM, SM],
        out_specs=VM,
        compiler_params=params(16),
        name="output",
    )(hist, self_term, gate, tokens, w, where, count)


def move(value, step, width=1):
    pairs = [(i, (i + (-step if i // width % 2 else step)) % NZ) for i in range(NZ)]
    return lax.ppermute(value, "z", pairs)


def swap(value):
    return lax.ppermute(value, "core", [(0, 1), (1, 0)])


def local(
    tokens,
    in_weight,
    out_weight,
    history_pool,
    position_bias,
    self_bias,
    history_length,
    candidate_count,
    block_slots,
    block_position,
):
    z, core, m = lax.axis_index("z"), lax.axis_index("core"), lax.axis_index(M)
    where = jnp.stack([z, core, m // 2, m]).astype(jnp.int32)
    length = history_length[:, None]
    mine = jnp.concatenate(
        [
            block_slots.reshape(1, NG * CAP),
            block_position.reshape(1, NG * CAP),
            length // 256,
            length % 256,
            jnp.zeros((1, 62), jnp.int32),
        ],
        axis=1,
    ).astype(jnp.bfloat16)
    mine = jnp.broadcast_to(mine, (16, 128))
    q, q_send = query(tokens, in_weight)
    q_mine = lax.all_to_all(q_send, M, split_axis=0, concat_axis=0, tiled=True)
    packed = pack(history_pool, q)
    q_mine, packed = lax.optimization_barrier((q_mine, packed))
    kv = lax.all_to_all(packed, M, split_axis=0, concat_axis=0, tiled=True)
    mine = jnp.concatenate([q_mine.reshape(HALF, HEAD), mine], axis=0)
    far_a, far_b = move(mine, 3), move(mine, -3)
    out_a, out_b = bundle(where, mine, far_a, far_b)
    q_own = stack(where, mine, far_a, far_b, move(out_a, 1), move(out_b, -1))
    q_other = swap(q_own)
    plan = table(where, q_own, q_other)
    gate, self_term, w2 = rest(tokens, in_weight, q, self_bias, out_weight)
    kv, gate, self_term, w2, plan = lax.optimization_barrier((kv, gate, self_term, w2, plan))
    own, other, blocks = attend_first(plan, where, position_bias, q_own, q_other, kv)
    other = swap(other)
    own = attend_second(plan, where, position_bias, q_own, blocks, own)
    out_a, out_b, half_a, half_b = far(where, own, other)
    side_a, side_b = side(where, own, other, out_a)
    side_a, side_b = move(side_a, 1), move(side_b, -1)
    half_a, half_b = move(half_a, 2, 2), move(half_b, -2, 2)
    out_a, out_b = near(where, own, other, move(out_a, 1), move(out_b, -1), half_a, half_b)
    hist = total(own, other, side_a, side_b, move(out_a, 2, 2), move(out_b, -2, 2))
    hist = lax.all_to_all(hist, M, split_axis=0, concat_axis=0, tiled=True)
    return tail(hist, self_term, gate, tokens, w2, where, candidate_count)


def solution(mesh):
    fine = Mesh(mesh.devices.reshape(NZ, 2, 4, 4), ("z", "core", "x", "y"))
    placed = (
        P(("z", "core", "x", "y"), None),
        P(),
        P(),
        P(("z", "core"), ("x", "y"), None),
        P(),
        P(),
        P(("z", "core")),
        P(("z", "core")),
        P(("z", "core"), None, None),
        P(("z", "core"), None, None),
    )
    return jax.shard_map(
        local, mesh=fine, in_specs=placed, out_specs=P(("z", "core", "x", "y"), None), check_vma=False
    )
```

```python
import functools

import jax
import jax.numpy as jnp
from jax import lax
from jax.experimental import pallas as pl
from jax.experimental.pallas import tpu as pltpu
from jax.sharding import Mesh, PartitionSpec as P

D = 1024
HEADS = 8
HEAD = 128
BLOCK = 512
BLK = 14
CAP = 2
NZ = 8
NG = 16
NM = 16
SLAB = 32
ROWS = 64
HALF = 512
QROWS = 528
CUT = 272
FIRST = 9
EPS = 1e-05
SCALE = HEAD**-0.5
G = ("z", "core")
M = ("half", "pair", "y")
W = ("pair", "y")
VM = pl.BlockSpec(memory_space=pltpu.VMEM)
SM = pl.BlockSpec(memory_space=pltpu.SMEM)
HB = pl.BlockSpec(memory_space=pltpu.HBM)


def params(mib):
    return pltpu.CompilerParams(vmem_limit_bytes=mib << 20)


def norm(values):
    center = values - jnp.mean(values, axis=-1, keepdims=True)
    spread = jnp.mean(center * center, axis=-1, keepdims=True)
    return center * lax.rsqrt(spread + EPS)


def silu(v):
    t = 0.5 * v
    return t + t * jnp.tanh(t)


def pack_kernel(pool, after, out):
    for h in range(HEADS):
        for kv in range(2):
            cols = pool[:, :, kv * D + h * HEAD : kv * D + (h + 1) * HEAD]
            for ch in range(2):
                out[ch * HEADS + h, kv] = cols


def pack(pool, after):
    return pl.pallas_call(
        pack_kernel,
        out_shape=jax.ShapeDtypeStruct((NM, 2, BLK, SLAB, HEAD), jnp.bfloat16),
        in_specs=[VM, VM],
        out_specs=VM,
        compiler_params=params(12),
        name="pack_history",
    )(pool, after)


def query_kernel(tokens, w, q_out, send_out, rows, buf, sems):
    first = pltpu.make_async_copy(tokens, rows, sems.at[4])
    first.start()
    copies = [
        pltpu.make_async_copy(w.at[:, pl.ds(2 * D + i * 256, 256)], buf.at[i], sems.at[i]) for i in range(4)
    ]
    for c in copies:
        c.start()
    first.wait()
    normed = norm(rows[...].astype(jnp.float32)).astype(jnp.bfloat16)
    for i in range(4):
        copies[i].wait()
        q = silu(jnp.dot(normed, buf[i], preferred_element_type=jnp.float32)).astype(jnp.bfloat16)
        q_out[:, i * 256 : (i + 1) * 256] = q
        for j in range(2):
            send_out[i * 2 + j] = q[:, j * HEAD : (j + 1) * HEAD]


def query(tokens, w):
    return pl.pallas_call(
        query_kernel,
        out_shape=(
            jax.ShapeDtypeStruct((ROWS, D), jnp.bfloat16),
            jax.ShapeDtypeStruct((HEADS, ROWS, HEAD), jnp.bfloat16),
        ),
        in_specs=[HB, HB],
        out_specs=(VM, VM),
        scratch_shapes=[
            pltpu.VMEM((ROWS, D), jnp.bfloat16),
            pltpu.VMEM((4, D, 256), jnp.bfloat16),
            pltpu.SemaphoreType.DMA((5,)),
        ],
        compiler_params=params(12),
        name="project_query",
    )(pltpu.with_memory_space_constraint(tokens, pltpu.HBM), pltpu.with_memory_space_constraint(w, pltpu.HBM))


def rest_kernel(tokens, w, q, self_bias, w2, gate_out, self_out, w2_out, buf, sems, sem):
    held = pltpu.make_async_copy(w2, w2_out, sem)
    held.start()
    copies = []
    for i in range(4):
        for j, base in enumerate((0, D, 3 * D)):
            n = i * 3 + j
            copies.append(
                pltpu.make_async_copy(w.at[:, pl.ds(base + i * 256, 256)], buf.at[n], sems.at[n])
            )
    for c in copies:
        c.start()
    normed = norm(tokens[...].astype(jnp.float32)).astype(jnp.bfloat16)

    def proj(n):
        copies[n].wait()
        return silu(jnp.dot(normed, buf[n], preferred_element_type=jnp.float32)).astype(jnp.bfloat16)

    for i in range(4):
        wide = slice(i * 256, (i + 1) * 256)
        gate_out[:, wide] = proj(i * 3)
        v = proj(i * 3 + 1).astype(jnp.float32)
        k = proj(i * 3 + 2).astype(jnp.float32)
        qk = q[:, wide].astype(jnp.float32) * k
        for j in range(2):
            cols = slice(j * HEAD, (j + 1) * HEAD)
            s = jnp.sum(qk[:, cols], axis=1, keepdims=True) * SCALE + self_bias[i * 2 + j]
            self_out[:, i * 256 + j * HEAD : i * 256 + (j + 1) * HEAD] = silu(s) * v[:, cols]
    held.wait()


def rest(tokens, w, q, self_bias, w2):
    return pl.pallas_call(
        rest_kernel,
        out_shape=(
            jax.ShapeDtypeStruct((ROWS, D), jnp.bfloat16),
            jax.ShapeDtypeStruct((ROWS, D), jnp.float32),
            pltpu.VMEM((D, D), jnp.bfloat16),
        ),
        in_specs=[VM, HB, VM, SM, HB],
        out_specs=(VM, VM, VM),
        scratch_shapes=[
            pltpu.VMEM((12, D, 256), jnp.bfloat16),
            pltpu.SemaphoreType.DMA((12,)),
            pltpu.SemaphoreType.DMA,
        ],
        compiler_params=params(20),
        name="project_rest",
    )(
        tokens,
        pltpu.with_memory_space_constraint(w, pltpu.HBM),
        q,
        self_bias,
        pltpu.with_memory_space_constraint(w2, pltpu.HBM),
    )


def by_side(where, body, first, second, width=1):
    even = lax.rem(lax.div(where[0], width), 2) == 0

    @pl.when(even)
    def _():
        body(*first, *second)

    @pl.when(jnp.logical_not(even))
    def _():
        body(*second, *first)


def bundle_kernel(where, own, far_a, far_b, out_a, out_b):
    def body(high, up, low, down):
        up[:QROWS] = own[...]
        up[QROWS : 2 * QROWS] = high[...]
        up[2 * QROWS :] = low[:CUT]
        down[:QROWS] = own[...]
        down[QROWS : 2 * QROWS] = low[...]
        down[2 * QROWS :] = high[QROWS - CUT :]

    by_side(where, body, (far_a, out_a), (far_b, out_b))


def bundle(*args):
    shape = jax.ShapeDtypeStruct((2 * QROWS + CUT, HEAD), jnp.bfloat16)
    return pl.pallas_call(
        bundle_kernel,
        out_shape=(shape, shape),
        in_specs=[SM] + [VM] * 3,
        out_specs=(VM, VM),
        compiler_params=params(12),
        name="bundle_queries",
    )(*args)


def stack_kernel(where, own, far_a, far_b, near_a, near_b, out):
    def body(high, plus, low, minus):
        out[0] = own[...]
        out[5] = low[...]
        out[3] = high[...]
        out[7] = minus[:QROWS]
        out[2] = minus[QROWS : 2 * QROWS]
        out[4, :CUT] = minus[2 * QROWS :]
        out[1] = plus[:QROWS]
        out[6] = plus[QROWS : 2 * QROWS]
        out[4, QROWS - CUT :] = plus[2 * QROWS :]

    by_side(where, body, (far_a, near_a), (far_b, near_b))


def stack(*args):
    return pl.pallas_call(
        stack_kernel,
        out_shape=jax.ShapeDtypeStruct((NZ, QROWS, HEAD), jnp.bfloat16),
        in_specs=[SM] + [VM] * 5,
        out_specs=VM,
        compiler_params=params(12),
        name="stack_queries",
    )(*args)


def table_kernel(where, q_own, q_other, plan, tab, ints, sem):
    o = where[0] * 2 + where[1]
    for i, q in enumerate((q_own, q_other)):
        for s in range(NZ):
            ints[i * NZ + s] = q[s, HALF:].astype(jnp.float32).astype(jnp.int32)[0:8]
    copy = pltpu.make_async_copy(ints.at[:, 0], tab, sem)
    copy.start()
    for i in range(4):
        for b in range(16):
            plan[i, b] = -1
    copy.wait()

    def step(row, carry):
        length = tab[row, 2 * NG * CAP] * 256 + tab[row, 2 * NG * CAP + 1]
        for c in range(CAP):
            slot = tab[row, o * CAP + c]

            @pl.when(slot >= 0)
            def _():
                p = tab[row, NG * CAP + o * CAP + c]
                plan[0, slot] = row
                plan[1, slot] = p
                plan[2, slot] = length - p * BLOCK

        return carry

    lax.fori_loop(0, NG, step, 0)
    budget = FIRST
    for b in range(BLK):
        budget -= (plan[0, b] >= NZ).astype(jnp.int32)
    for b in range(BLK):
        row = plan[0, b]
        mine = (row >= 0) & (row < NZ)
        later = mine & (budget <= 0)
        budget -= mine.astype(jnp.int32)
        plan[3, b] = jnp.where(row < 0, -1, jnp.where(later, 1, 0))


def table(where, q_own, q_other):
    return pl.pallas_call(
        table_kernel,
        out_shape=jax.ShapeDtypeStruct((4, 16), jnp.int32),
        in_specs=[SM, VM, VM],
        out_specs=SM,
        scratch_shapes=[
            pltpu.SMEM((NG, 128), jnp.int32),
            pltpu.VMEM((NG, 8, 128), jnp.int32),
            pltpu.SemaphoreType.DMA,
        ],
        compiler_params=params(12),
        name="read_tables",
    )(where, q_own, q_other)


def attend_blocks(phase, plan, where, bias, pick, blocks, ready, acc):
    h = where[2]
    for b in range(BLK):
        ready(b)

        @pl.when(plan[3, b] == phase)
        def _():
            row = plan[0, b]
            keys = blocks[b, :, 0].reshape(BLOCK, HEAD)
            values = blocks[b, :, 1].reshape(BLOCK, HEAD)
            token = lax.broadcasted_iota(jnp.int32, (BLOCK, HEAD), 0)
            values = jnp.where(token < plan[2, b], values, jnp.zeros_like(values))
            scores = lax.dot_general(
                pick(row), keys, (((1,), (1,)), ((), ())), preferred_element_type=jnp.float32
            )
            t = scores * (0.5 * SCALE) + bias[h, plan[1, b]] * 0.5
            weights = (t + t * jnp.tanh(t)).astype(jnp.bfloat16)
            acc[row] += jnp.dot(weights, values, preferred_element_type=jnp.float32)


def first_kernel(plan, where, bias, q_own, q_other, kv, own, other, blocks, acc, sems):
    copies = [pltpu.make_async_copy(kv.at[:, :, b], blocks.at[b], sems.at[b]) for b in range(BLK)]
    for c in copies:
        c.start()
    acc[...] = jnp.zeros_like(acc)

    def pick(row):
        return jnp.where(row < NZ, q_own[lax.rem(row, NZ), :HALF], q_other[lax.rem(row, NZ), :HALF])

    attend_blocks(0, plan, where, bias, pick, blocks, lambda b: copies[b].wait(), acc)
    own[...] = acc[:NZ]
    other[...] = acc[NZ:].astype(jnp.bfloat16)


def second_kernel(plan, where, bias, q, blocks, own, out, acc):
    acc[...] = own[...]
    attend_blocks(1, plan, where, bias, lambda row: q[row, :HALF], blocks, lambda b: None, acc)
    out[...] = acc[...].astype(jnp.bfloat16)


def attend_first(plan, where, bias, q_own, q_other, kv):
    return pl.pallas_call(
        first_kernel,
        out_shape=(
            jax.ShapeDtypeStruct((NZ, HALF, HEAD), jnp.float32),
            jax.ShapeDtypeStruct((NZ, HALF, HEAD), jnp.bfloat16),
            jax.ShapeDtypeStruct((BLK, NM, 2, SLAB, HEAD), jnp.bfloat16),
        ),
        in_specs=[SM, SM, SM, VM, VM, HB],
        out_specs=(VM, VM, VM),
        scratch_shapes=[pltpu.VMEM((NG, HALF, HEAD), jnp.float32), pltpu.SemaphoreType.DMA((BLK,))],
        compiler_params=params(20),
        name="attend_first",
    )(plan, where, bias, q_own, q_other, pltpu.with_memory_space_constraint(kv, pltpu.HBM))


def attend_second(plan, where, bias, q, blocks, own):
    return pl.pallas_call(
        second_kernel,
        out_shape=jax.ShapeDtypeStruct((NZ, HALF, HEAD), jnp.bfloat16),
        in_specs=[SM, SM, SM, VM, VM, VM],
        out_specs=VM,
        scratch_shapes=[pltpu.VMEM((NZ, HALF, HEAD), jnp.float32)],
        compiler_params=params(16),
        name="attend_second",
    )(plan, where, bias, q, blocks, own)


def add(*refs):
    total = refs[0].astype(jnp.float32)
    for r in refs[1:]:
        total += r.astype(jnp.float32)
    return total


def far_kernel(where, a, b, out_a, out_b, half_a, half_b):
    def body(up, down):
        up[...] = add(a[3], b[3]).astype(jnp.bfloat16)
        down[...] = add(a[5], b[5]).astype(jnp.bfloat16)

    def opposite(up, down):
        up[...] = add(a[4, :256], b[4, :256]).astype(jnp.bfloat16)
        down[...] = add(a[4, 256:], b[4, 256:]).astype(jnp.bfloat16)

    by_side(where, body, (out_a,), (out_b,))
    by_side(where, opposite, (half_a,), (half_b,), 2)


def far(*args):
    part = jax.ShapeDtypeStruct((HALF, HEAD), jnp.bfloat16)
    half = jax.ShapeDtypeStruct((256, HEAD), jnp.bfloat16)
    return pl.pallas_call(
        far_kernel,
        out_shape=(part, part, half, half),
        in_specs=[SM] + [VM] * 2,
        out_specs=(VM,) * 4,
        compiler_params=params(12),
        name="add_far",
    )(*args)


def side_kernel(where, a, b, after, out_a, out_b):
    def body(up, down):
        up[...] = add(a[1], b[1]).astype(jnp.bfloat16)
        down[...] = add(a[7], b[7]).astype(jnp.bfloat16)

    by_side(where, body, (out_a,), (out_b,))


def side(*args):
    part = jax.ShapeDtypeStruct((HALF, HEAD), jnp.bfloat16)
    return pl.pallas_call(
        side_kernel,
        out_shape=(part, part),
        in_specs=[SM] + [VM] * 3,
        out_specs=(VM,) * 2,
        compiler_params=params(12),
        name="add_side",
    )(*args)


def near_kernel(where, a, b, near_a, near_b, half_a, half_b, out_a, out_b, ups, downs):
    def body(plus, minus):
        ups[...] = add(a[2], b[2], minus[...])
        downs[...] = add(a[6], b[6], plus[...])

    def opposite(plus, up, minus, down):
        up[:256] = add(ups[:256], minus[...]).astype(jnp.bfloat16)
        up[256:] = ups[256:].astype(jnp.bfloat16)
        down[:256] = downs[:256].astype(jnp.bfloat16)
        down[256:] = add(downs[256:], plus[...]).astype(jnp.bfloat16)

    by_side(where, body, (near_a,), (near_b,))
    by_side(where, opposite, (half_a, out_a), (half_b, out_b), 2)


def near(*args):
    part = jax.ShapeDtypeStruct((HALF, HEAD), jnp.bfloat16)
    return pl.pallas_call(
        near_kernel,
        out_shape=(part, part),
        in_specs=[SM] + [VM] * 6,
        out_specs=(VM,) * 2,
        scratch_shapes=[pltpu.VMEM((HALF, HEAD), jnp.float32)] * 2,
        compiler_params=params(12),
        name="add_near",
    )(*args)


def total_kernel(own, other, *refs):
    total = add(own[0], other[0], *(r[...] for r in refs[:-1]))
    refs[-1][...] = total.astype(jnp.bfloat16).reshape(HEADS, ROWS, HEAD)


def total(*parts):
    return pl.pallas_call(
        total_kernel,
        out_shape=jax.ShapeDtypeStruct((HEADS, ROWS, HEAD), jnp.bfloat16),
        in_specs=[VM] * 6,
        out_specs=VM,
        compiler_params=params(12),
        name="add_groups",
    )(*parts)


def tail_kernel(hist, self_term, gate, tokens, w, where, count, out):
    attended = jnp.concatenate([hist[h] for h in range(HEADS)], axis=1).astype(jnp.float32) + self_term[...]
    gated = (norm(attended) * gate[...].astype(jnp.float32)).astype(jnp.bfloat16)
    res = jnp.dot(gated, w[...], preferred_element_type=jnp.float32) + tokens[...].astype(jnp.float32)
    row = where[3] * ROWS + lax.broadcasted_iota(jnp.int32, (ROWS, D), 0)
    out[...] = jnp.where(row < count[0], res, 0.0).astype(jnp.bfloat16)


def tail(hist, self_term, gate, tokens, w, where, count):
    return pl.pallas_call(
        tail_kernel,
        out_shape=jax.ShapeDtypeStruct((ROWS, D), jnp.bfloat16),
        in_specs=[VM, VM, VM, VM, VM, SM, SM],
        out_specs=VM,
        compiler_params=params(16),
        name="output",
    )(hist, self_term, gate, tokens, w, where, count)


def move(value, step, width=1):
    pairs = [(i, (i + (-step if i // width % 2 else step)) % NZ) for i in range(NZ)]
    return lax.ppermute(value, "z", pairs)


def swap(value):
    return lax.ppermute(value, "core", [(0, 1), (1, 0)])


def local(
    tokens,
    in_weight,
    out_weight,
    history_pool,
    position_bias,
    self_bias,
    history_length,
    candidate_count,
    block_slots,
    block_position,
):
    z, core, m = lax.axis_index("z"), lax.axis_index("core"), lax.axis_index(M)
    where = jnp.stack([z, core, m % HEADS, m]).astype(jnp.int32)
    length = history_length[:, None]
    mine = jnp.concatenate(
        [
            block_slots.reshape(1, NG * CAP),
            block_position.reshape(1, NG * CAP),
            length // 256,
            length % 256,
            jnp.zeros((1, 62), jnp.int32),
        ],
        axis=1,
    ).astype(jnp.bfloat16)
    mine = jnp.broadcast_to(mine, (16, 128))
    q, q_send = query(tokens, in_weight)
    q_mine = lax.all_to_all(q_send, W, split_axis=0, concat_axis=0, tiled=True)
    packed = pack(history_pool, q)
    q_mine, packed = lax.optimization_barrier((q_mine, packed))
    kv = lax.all_to_all(packed, M, split_axis=0, concat_axis=0, tiled=True)
    mine = jnp.concatenate([q_mine.reshape(HALF, HEAD), mine], axis=0)
    far_a, far_b = move(mine, 3), move(mine, -3)
    out_a, out_b = bundle(where, mine, far_a, far_b)
    q_own = stack(where, mine, far_a, far_b, move(out_a, 1), move(out_b, -1))
    q_other = swap(q_own)
    plan = table(where, q_own, q_other)
    gate, self_term, w2 = rest(tokens, in_weight, q, self_bias, out_weight)
    kv, gate, self_term, w2, plan = lax.optimization_barrier((kv, gate, self_term, w2, plan))
    own, other, blocks = attend_first(plan, where, position_bias, q_own, q_other, kv)
    other = swap(other)
    own = attend_second(plan, where, position_bias, q_own, blocks, own)
    out_a, out_b, half_a, half_b = far(where, own, other)
    side_a, side_b = side(where, own, other, out_a)
    side_a, side_b = move(side_a, 1), move(side_b, -1)
    half_a, half_b = move(half_a, 2, 2), move(half_b, -2, 2)
    out_a, out_b = near(where, own, other, move(out_a, 1), move(out_b, -1), half_a, half_b)
    hist = total(own, other, side_a, side_b, move(out_a, 2, 2), move(out_b, -2, 2))
    hist = lax.all_to_all(hist, W, split_axis=0, concat_axis=0, tiled=True)
    return tail(hist, self_term, gate, tokens, w2, where, candidate_count)


def solution(mesh):
    names = ("z", "core", "half", "pair", "y")
    fine = Mesh(mesh.devices.reshape(NZ, 2, 2, 2, 4), names)
    placed = (
        P(names, None),
        P(),
        P(),
        P(G, M, None),
        P(),
        P(),
        P(G),
        P(G),
        P(G, None, None),
        P(G, None, None),
    )
    return jax.shard_map(
        local, mesh=fine, in_specs=placed, out_specs=P(names, None), check_vma=False
    )
```

```python
import functools

import jax
import jax.numpy as jnp
from jax import lax
from jax.experimental import pallas as pl
from jax.experimental.pallas import tpu as pltpu
from jax.sharding import Mesh, PartitionSpec as P

D = 1024
HEADS = 8
HEAD = 128
BLOCK = 512
BLK = 14
CAP = 2
NZ = 8
NG = 16
NM = 16
SLAB = 32
ROWS = 64
HALF = 512
QROWS = 528
CUT = 272
FIRST = 9
EPS = 1e-05
SCALE = HEAD**-0.5
G = ("z", "core")
M = ("half", "pair", "y")
W = ("pair", "y")
VM = pl.BlockSpec(memory_space=pltpu.VMEM)
SM = pl.BlockSpec(memory_space=pltpu.SMEM)
HB = pl.BlockSpec(memory_space=pltpu.HBM)


def params(mib):
    return pltpu.CompilerParams(vmem_limit_bytes=mib << 20)


def norm(values):
    center = values - jnp.mean(values, axis=-1, keepdims=True)
    spread = jnp.mean(center * center, axis=-1, keepdims=True)
    return center * lax.rsqrt(spread + EPS)


def silu(v):
    t = 0.5 * v
    return t + t * jnp.tanh(t)


def pack_kernel(pool, after, out):
    for h in range(HEADS):
        for kv in range(2):
            cols = pool[:, :, kv * D + h * HEAD : kv * D + (h + 1) * HEAD]
            for ch in range(2):
                out[ch * HEADS + h, kv] = cols


def pack(pool, after):
    return pl.pallas_call(
        pack_kernel,
        out_shape=jax.ShapeDtypeStruct((NM, 2, BLK, SLAB, HEAD), jnp.bfloat16),
        in_specs=[VM, VM],
        out_specs=VM,
        compiler_params=params(12),
        name="pack_history",
    )(pool, after)


def query_kernel(tokens, w, q_out, send_out, rows, buf, send, sems):
    first = pltpu.make_async_copy(tokens, rows, sems.at[4])
    first.start()
    copies = [
        pltpu.make_async_copy(w.at[:, pl.ds(2 * D + i * 256, 256)], buf.at[i], sems.at[i]) for i in range(4)
    ]
    for c in copies:
        c.start()
    first.wait()
    normed = norm(rows[...].astype(jnp.float32)).astype(jnp.bfloat16)
    moves = []
    for i in range(4):
        copies[i].wait()
        q = silu(jnp.dot(normed, buf[i], preferred_element_type=jnp.float32)).astype(jnp.bfloat16)
        for j in range(2):
            send[i * 2 + j] = q[:, j * HEAD : (j + 1) * HEAD]
        two = pl.ds(i * 2, 2)
        moves.append(pltpu.make_async_copy(send.at[two], send_out.at[two], sems.at[5 + i]))
        moves[i].start()
        q_out[:, i * 256 : (i + 1) * 256] = q
    for c in moves:
        c.wait()


def query(tokens, w):
    return pl.pallas_call(
        query_kernel,
        out_shape=(
            jax.ShapeDtypeStruct((ROWS, D), jnp.bfloat16),
            jax.ShapeDtypeStruct((HEADS, ROWS, HEAD), jnp.bfloat16),
        ),
        in_specs=[HB, HB],
        out_specs=(VM, HB),
        scratch_shapes=[
            pltpu.VMEM((ROWS, D), jnp.bfloat16),
            pltpu.VMEM((4, D, 256), jnp.bfloat16),
            pltpu.VMEM((HEADS, ROWS, HEAD), jnp.bfloat16),
            pltpu.SemaphoreType.DMA((9,)),
        ],
        compiler_params=params(12),
        name="project_query",
    )(pltpu.with_memory_space_constraint(tokens, pltpu.HBM), pltpu.with_memory_space_constraint(w, pltpu.HBM))


def rest_kernel(tokens, w, q, self_bias, w2, gate_out, self_out, w2_out, buf, sems, sem):
    held = pltpu.make_async_copy(w2, w2_out, sem)
    held.start()
    copies = []
    for i in range(4):
        for j, base in enumerate((0, D, 3 * D)):
            n = i * 3 + j
            copies.append(
                pltpu.make_async_copy(w.at[:, pl.ds(base + i * 256, 256)], buf.at[n], sems.at[n])
            )
    for c in copies:
        c.start()
    normed = norm(tokens[...].astype(jnp.float32)).astype(jnp.bfloat16)

    def proj(n):
        copies[n].wait()
        return silu(jnp.dot(normed, buf[n], preferred_element_type=jnp.float32)).astype(jnp.bfloat16)

    for i in range(4):
        wide = slice(i * 256, (i + 1) * 256)
        gate_out[:, wide] = proj(i * 3)
        v = proj(i * 3 + 1).astype(jnp.float32)
        k = proj(i * 3 + 2).astype(jnp.float32)
        qk = q[:, wide].astype(jnp.float32) * k
        for j in range(2):
            cols = slice(j * HEAD, (j + 1) * HEAD)
            s = jnp.sum(qk[:, cols], axis=1, keepdims=True) * SCALE + self_bias[i * 2 + j]
            self_out[:, i * 256 + j * HEAD : i * 256 + (j + 1) * HEAD] = silu(s) * v[:, cols]
    held.wait()


def rest(tokens, w, q, self_bias, w2):
    return pl.pallas_call(
        rest_kernel,
        out_shape=(
            jax.ShapeDtypeStruct((ROWS, D), jnp.bfloat16),
            jax.ShapeDtypeStruct((ROWS, D), jnp.float32),
            pltpu.VMEM((D, D), jnp.bfloat16),
        ),
        in_specs=[VM, HB, VM, SM, HB],
        out_specs=(VM, VM, VM),
        scratch_shapes=[
            pltpu.VMEM((12, D, 256), jnp.bfloat16),
            pltpu.SemaphoreType.DMA((12,)),
            pltpu.SemaphoreType.DMA,
        ],
        compiler_params=params(20),
        name="project_rest",
    )(
        tokens,
        pltpu.with_memory_space_constraint(w, pltpu.HBM),
        q,
        self_bias,
        pltpu.with_memory_space_constraint(w2, pltpu.HBM),
    )


def by_side(where, body, first, second, width=1):
    even = lax.rem(lax.div(where[0], width), 2) == 0

    @pl.when(even)
    def _():
        body(*first, *second)

    @pl.when(jnp.logical_not(even))
    def _():
        body(*second, *first)


def bundle_kernel(where, own, far_a, far_b, out_a, out_b):
    def body(high, up, low, down):
        up[:QROWS] = own[...]
        up[QROWS : 2 * QROWS] = high[...]
        up[2 * QROWS :] = low[:CUT]
        down[:QROWS] = own[...]
        down[QROWS : 2 * QROWS] = low[...]
        down[2 * QROWS :] = high[QROWS - CUT :]

    by_side(where, body, (far_a, out_a), (far_b, out_b))


def bundle(*args):
    shape = jax.ShapeDtypeStruct((2 * QROWS + CUT, HEAD), jnp.bfloat16)
    return pl.pallas_call(
        bundle_kernel,
        out_shape=(shape, shape),
        in_specs=[SM] + [VM] * 3,
        out_specs=(VM, VM),
        compiler_params=params(12),
        name="bundle_queries",
    )(*args)


def stack_kernel(where, own, far_a, far_b, near_a, near_b, out):
    def body(high, plus, low, minus):
        out[0] = own[...]
        out[5] = low[...]
        out[3] = high[...]
        out[7] = minus[:QROWS]
        out[2] = minus[QROWS : 2 * QROWS]
        out[4, :CUT] = minus[2 * QROWS :]
        out[1] = plus[:QROWS]
        out[6] = plus[QROWS : 2 * QROWS]
        out[4, QROWS - CUT :] = plus[2 * QROWS :]

    by_side(where, body, (far_a, near_a), (far_b, near_b))


def stack(*args):
    return pl.pallas_call(
        stack_kernel,
        out_shape=jax.ShapeDtypeStruct((NZ, QROWS, HEAD), jnp.bfloat16),
        in_specs=[SM] + [VM] * 5,
        out_specs=VM,
        compiler_params=params(12),
        name="stack_queries",
    )(*args)


def table_kernel(where, q_own, q_other, plan, tab, ints, sem):
    o = where[0] * 2 + where[1]
    for i, q in enumerate((q_own, q_other)):
        for s in range(NZ):
            ints[i * NZ + s] = q[s, HALF:].astype(jnp.float32).astype(jnp.int32)[0:8]
    copy = pltpu.make_async_copy(ints.at[:, 0], tab, sem)
    copy.start()
    for i in range(4):
        for b in range(16):
            plan[i, b] = -1
    copy.wait()

    def step(row, carry):
        length = tab[row, 2 * NG * CAP] * 256 + tab[row, 2 * NG * CAP + 1]
        for c in range(CAP):
            slot = tab[row, o * CAP + c]

            @pl.when(slot >= 0)
            def _():
                p = tab[row, NG * CAP + o * CAP + c]
                plan[0, slot] = row
                plan[1, slot] = p
                plan[2, slot] = length - p * BLOCK

        return carry

    lax.fori_loop(0, NG, step, 0)
    budget = FIRST
    for b in range(BLK):
        budget -= (plan[0, b] >= NZ).astype(jnp.int32)
    for b in range(BLK):
        row = plan[0, b]
        mine = (row >= 0) & (row < NZ)
        later = mine & (budget <= 0)
        budget -= mine.astype(jnp.int32)
        plan[3, b] = jnp.where(row < 0, -1, jnp.where(later, 1, 0))


def table(where, q_own, q_other):
    return pl.pallas_call(
        table_kernel,
        out_shape=jax.ShapeDtypeStruct((4, 16), jnp.int32),
        in_specs=[SM, VM, VM],
        out_specs=SM,
        scratch_shapes=[
            pltpu.SMEM((NG, 128), jnp.int32),
            pltpu.VMEM((NG, 8, 128), jnp.int32),
            pltpu.SemaphoreType.DMA,
        ],
        compiler_params=params(12),
        name="read_tables",
    )(where, q_own, q_other)


def attend_blocks(phase, plan, where, bias, pick, blocks, ready, acc):
    h = where[2]
    for b in range(BLK):
        ready(b)

        @pl.when(plan[3, b] == phase)
        def _():
            row = plan[0, b]
            keys = blocks[b, :, 0].reshape(BLOCK, HEAD)
            values = blocks[b, :, 1].reshape(BLOCK, HEAD)
            token = lax.broadcasted_iota(jnp.int32, (BLOCK, HEAD), 0)
            values = jnp.where(token < plan[2, b], values, jnp.zeros_like(values))
            scores = lax.dot_general(
                pick(row), keys, (((1,), (1,)), ((), ())), preferred_element_type=jnp.float32
            )
            t = scores * (0.5 * SCALE) + bias[h, plan[1, b]] * 0.5
            weights = (t + t * jnp.tanh(t)).astype(jnp.bfloat16)
            acc[row] += jnp.dot(weights, values, preferred_element_type=jnp.float32)


def first_kernel(plan, where, bias, q_own, q_other, kv, own, other, blocks, acc, sems):
    copies = [pltpu.make_async_copy(kv.at[:, :, b], blocks.at[b], sems.at[b]) for b in range(BLK)]
    for c in copies[:2]:
        c.start()
    acc[...] = jnp.zeros_like(acc)
    for c in copies[2:]:
        c.start()

    def pick(row):
        return jnp.where(row < NZ, q_own[lax.rem(row, NZ), :HALF], q_other[lax.rem(row, NZ), :HALF])

    attend_blocks(0, plan, where, bias, pick, blocks, lambda b: copies[b].wait(), acc)
    own[...] = acc[:NZ]
    other[...] = acc[NZ:].astype(jnp.bfloat16)


def second_kernel(plan, where, bias, q, blocks, own, out, acc):
    acc[...] = own[...]
    attend_blocks(1, plan, where, bias, lambda row: q[row, :HALF], blocks, lambda b: None, acc)
    out[...] = acc[...].astype(jnp.bfloat16)


def attend_first(plan, where, bias, q_own, q_other, kv):
    return pl.pallas_call(
        first_kernel,
        out_shape=(
            jax.ShapeDtypeStruct((NZ, HALF, HEAD), jnp.float32),
            jax.ShapeDtypeStruct((NZ, HALF, HEAD), jnp.bfloat16),
            jax.ShapeDtypeStruct((BLK, NM, 2, SLAB, HEAD), jnp.bfloat16),
        ),
        in_specs=[SM, SM, SM, VM, VM, HB],
        out_specs=(VM, VM, VM),
        scratch_shapes=[pltpu.VMEM((NG, HALF, HEAD), jnp.float32), pltpu.SemaphoreType.DMA((BLK,))],
        compiler_params=params(20),
        name="attend_first",
    )(plan, where, bias, q_own, q_other, pltpu.with_memory_space_constraint(kv, pltpu.HBM))


def attend_second(plan, where, bias, q, blocks, own):
    return pl.pallas_call(
        second_kernel,
        out_shape=jax.ShapeDtypeStruct((NZ, HALF, HEAD), jnp.bfloat16),
        in_specs=[SM, SM, SM, VM, VM, VM],
        out_specs=VM,
        scratch_shapes=[pltpu.VMEM((NZ, HALF, HEAD), jnp.float32)],
        compiler_params=params(16),
        name="attend_second",
    )(plan, where, bias, q, blocks, own)


def add(*refs):
    total = refs[0].astype(jnp.float32)
    for r in refs[1:]:
        total += r.astype(jnp.float32)
    return total


def far_kernel(where, a, b, out_a, out_b, across):
    def body(up, down):
        up[...] = add(a[3], b[3]).astype(jnp.bfloat16)
        down[...] = add(a[5], b[5]).astype(jnp.bfloat16)

    by_side(where, body, (out_a,), (out_b,))
    across[...] = add(a[4], b[4]).astype(jnp.bfloat16)


def far(*args):
    part = jax.ShapeDtypeStruct((HALF, HEAD), jnp.bfloat16)
    return pl.pallas_call(
        far_kernel,
        out_shape=(part,) * 3,
        in_specs=[SM] + [VM] * 2,
        out_specs=(VM,) * 3,
        compiler_params=params(12),
        name="add_far",
    )(*args)


def side_kernel(where, a, b, after, out_a, out_b):
    def body(up, down):
        up[...] = add(a[1], b[1]).astype(jnp.bfloat16)
        down[...] = add(a[7], b[7]).astype(jnp.bfloat16)

    by_side(where, body, (out_a,), (out_b,))


def side(*args):
    part = jax.ShapeDtypeStruct((HALF, HEAD), jnp.bfloat16)
    return pl.pallas_call(
        side_kernel,
        out_shape=(part, part),
        in_specs=[SM] + [VM] * 3,
        out_specs=(VM,) * 2,
        compiler_params=params(12),
        name="add_side",
    )(*args)


def near_kernel(where, a, b, near_a, near_b, across, out_a, out_b):
    rising = lax.rem(lax.div(where[0], 2), 2) == 0
    goes_up = rising == (where[1] == 1)

    def width(up, down):
        def body(ahead, behind):
            moved = across[...].astype(jnp.float32)
            none = jnp.zeros_like(moved)
            up[...] = add(a[2], b[2], behind[...], jnp.where(goes_up, moved, none)).astype(jnp.bfloat16)
            down[...] = add(a[6], b[6], ahead[...], jnp.where(goes_up, none, moved)).astype(jnp.bfloat16)

        by_side(where, body, (near_a,), (near_b,))

    by_side(where, width, (out_a,), (out_b,), 2)


def near(*args):
    part = jax.ShapeDtypeStruct((HALF, HEAD), jnp.bfloat16)
    return pl.pallas_call(
        near_kernel,
        out_shape=(part, part),
        in_specs=[SM] + [VM] * 5,
        out_specs=(VM,) * 2,
        compiler_params=params(12),
        name="add_near",
    )(*args)


def total_kernel(own, other, *refs):
    total = add(own[0], other[0], *(r[...] for r in refs[:-1]))
    refs[-1][...] = total.astype(jnp.bfloat16).reshape(HEADS, ROWS, HEAD)


def total(*parts):
    return pl.pallas_call(
        total_kernel,
        out_shape=jax.ShapeDtypeStruct((HEADS, ROWS, HEAD), jnp.bfloat16),
        in_specs=[VM] * 6,
        out_specs=VM,
        compiler_params=params(12),
        name="add_groups",
    )(*parts)


def tail_kernel(hist, self_term, gate, tokens, w, where, count, out):
    attended = jnp.concatenate([hist[h] for h in range(HEADS)], axis=1).astype(jnp.float32) + self_term[...]
    gated = (norm(attended) * gate[...].astype(jnp.float32)).astype(jnp.bfloat16)
    res = jnp.dot(gated, w[...], preferred_element_type=jnp.float32) + tokens[...].astype(jnp.float32)
    row = where[3] * ROWS + lax.broadcasted_iota(jnp.int32, (ROWS, D), 0)
    out[...] = jnp.where(row < count[0], res, 0.0).astype(jnp.bfloat16)


def tail(hist, self_term, gate, tokens, w, where, count):
    return pl.pallas_call(
        tail_kernel,
        out_shape=jax.ShapeDtypeStruct((ROWS, D), jnp.bfloat16),
        in_specs=[VM, VM, VM, VM, VM, SM, SM],
        out_specs=VM,
        compiler_params=params(16),
        name="output",
    )(hist, self_term, gate, tokens, w, where, count)


def move(value, step, width=1):
    pairs = [(i, (i + (-step if i // width % 2 else step)) % NZ) for i in range(NZ)]
    return lax.ppermute(value, "z", pairs)


def cross(value):
    pairs = []
    for i in range(NG):
        step = 2 if (i // 4 + i) % 2 == 0 else -2
        pairs.append((i, (i // 2 + step) % NZ * 2 + i % 2))
    return lax.ppermute(value, G, pairs)


def swap(value):
    return lax.ppermute(value, "core", [(0, 1), (1, 0)])


def local(
    tokens,
    in_weight,
    out_weight,
    history_pool,
    position_bias,
    self_bias,
    history_length,
    candidate_count,
    block_slots,
    block_position,
):
    z, core, m = lax.axis_index("z"), lax.axis_index("core"), lax.axis_index(M)
    where = jnp.stack([z, core, m % HEADS, m]).astype(jnp.int32)
    length = history_length[:, None]
    mine = jnp.concatenate(
        [
            block_slots.reshape(1, NG * CAP),
            block_position.reshape(1, NG * CAP),
            length // 256,
            length % 256,
            jnp.zeros((1, 62), jnp.int32),
        ],
        axis=1,
    ).astype(jnp.bfloat16)
    mine = jnp.broadcast_to(mine, (16, 128))
    q, q_send = query(tokens, in_weight)
    q_mine = lax.all_to_all(q_send, W, split_axis=0, concat_axis=0, tiled=True)
    packed = pack(history_pool, q)
    q_mine, packed = lax.optimization_barrier((q_mine, packed))
    kv = lax.all_to_all(packed, M, split_axis=0, concat_axis=0, tiled=True)
    mine = jnp.concatenate([q_mine.reshape(HALF, HEAD), mine], axis=0)
    far_a, far_b = move(mine, 3), move(mine, -3)
    out_a, out_b = bundle(where, mine, far_a, far_b)
    q_own = stack(where, mine, far_a, far_b, move(out_a, 1), move(out_b, -1))
    q_other = swap(q_own)
    plan = table(where, q_own, q_other)
    gate, self_term, w2 = rest(tokens, in_weight, q, self_bias, out_weight)
    kv, gate, self_term, w2, plan = lax.optimization_barrier((kv, gate, self_term, w2, plan))
    own, other, blocks = attend_first(plan, where, position_bias, q_own, q_other, kv)
    other = swap(other)
    own = attend_second(plan, where, position_bias, q_own, blocks, own)
    out_a, out_b, across = far(where, own, other)
    side_a, side_b = side(where, own, other, out_a)
    side_a, side_b = move(side_a, 1), move(side_b, -1)
    out_a, out_b = near(where, own, other, move(out_a, 1), move(out_b, -1), cross(across))
    hist = total(own, other, side_a, side_b, move(out_a, 2, 2), move(out_b, -2, 2))
    hist = lax.all_to_all(hist, W, split_axis=0, concat_axis=0, tiled=True)
    return tail(hist, self_term, gate, tokens, w2, where, candidate_count)


def solution(mesh):
    names = ("z", "core", "half", "pair", "y")
    fine = Mesh(mesh.devices.reshape(NZ, 2, 2, 2, 4), names)
    placed = (
        P(names, None),
        P(),
        P(),
        P(G, M, None),
        P(),
        P(),
        P(G),
        P(G),
        P(G, None, None),
        P(G, None, None),
    )
    return jax.shard_map(
        local, mesh=fine, in_specs=placed, out_specs=P(names, None), check_vma=False
    )
```

```python
import functools

import jax
import jax.numpy as jnp
from jax import lax
from jax.experimental import pallas as pl
from jax.experimental.pallas import tpu as pltpu
from jax.sharding import Mesh, PartitionSpec as P

D = 1024
HEADS = 8
HEAD = 128
BLOCK = 512
BLK = 14
CAP = 2
NZ = 8
NG = 16
NM = 16
SLAB = 32
ROWS = 64
HALF = 512
QROWS = 528
CUT = 272
FIRST = 9
EPS = 1e-05
SCALE = HEAD**-0.5
G = ("z", "core")
M = ("half", "pair", "y")
W = ("pair", "y")
VM = pl.BlockSpec(memory_space=pltpu.VMEM)
SM = pl.BlockSpec(memory_space=pltpu.SMEM)
HB = pl.BlockSpec(memory_space=pltpu.HBM)


def params(mib):
    return pltpu.CompilerParams(vmem_limit_bytes=mib << 20)


def norm(values):
    center = values - jnp.mean(values, axis=-1, keepdims=True)
    spread = jnp.mean(center * center, axis=-1, keepdims=True)
    return center * lax.rsqrt(spread + EPS)


def silu(v):
    t = 0.5 * v
    return t + t * jnp.tanh(t)


def pack_kernel(pool, after, out):
    for h in range(HEADS):
        for kv in range(2):
            cols = pool[:, :, kv * D + h * HEAD : kv * D + (h + 1) * HEAD]
            for ch in range(2):
                out[ch * HEADS + h, kv] = cols


def pack(pool, after):
    return pl.pallas_call(
        pack_kernel,
        out_shape=jax.ShapeDtypeStruct((NM, 2, BLK, SLAB, HEAD), jnp.bfloat16),
        in_specs=[VM, VM],
        out_specs=VM,
        compiler_params=params(12),
        name="pack_history",
    )(pool, after)


def query_kernel(tokens, w, q_out, send_out, rows, buf, send, sems):
    first = pltpu.make_async_copy(tokens, rows, sems.at[4])
    first.start()
    copies = [
        pltpu.make_async_copy(w.at[:, pl.ds(2 * D + i * 256, 256)], buf.at[i], sems.at[i]) for i in range(4)
    ]
    for c in copies:
        c.start()
    first.wait()
    normed = norm(rows[...].astype(jnp.float32)).astype(jnp.bfloat16)
    moves = []
    for i in range(4):
        copies[i].wait()
        q = silu(jnp.dot(normed, buf[i], preferred_element_type=jnp.float32)).astype(jnp.bfloat16)
        for j in range(2):
            send[i * 2 + j] = q[:, j * HEAD : (j + 1) * HEAD]
        two = pl.ds(i * 2, 2)
        moves.append(pltpu.make_async_copy(send.at[two], send_out.at[two], sems.at[5 + i]))
        moves[i].start()
        q_out[:, i * 256 : (i + 1) * 256] = q
    for c in moves:
        c.wait()


def query(tokens, w):
    return pl.pallas_call(
        query_kernel,
        out_shape=(
            jax.ShapeDtypeStruct((ROWS, D), jnp.bfloat16),
            jax.ShapeDtypeStruct((HEADS, ROWS, HEAD), jnp.bfloat16),
        ),
        in_specs=[HB, HB],
        out_specs=(VM, HB),
        scratch_shapes=[
            pltpu.VMEM((ROWS, D), jnp.bfloat16),
            pltpu.VMEM((4, D, 256), jnp.bfloat16),
            pltpu.VMEM((HEADS, ROWS, HEAD), jnp.bfloat16),
            pltpu.SemaphoreType.DMA((9,)),
        ],
        compiler_params=params(12),
        name="project_query",
    )(pltpu.with_memory_space_constraint(tokens, pltpu.HBM), pltpu.with_memory_space_constraint(w, pltpu.HBM))


def rest_kernel(tokens, w, q, self_bias, w2, gate_out, self_out, w2_out, buf, sems, sem):
    held = pltpu.make_async_copy(w2, w2_out, sem)
    held.start()
    copies = []
    for i in range(4):
        for j, base in enumerate((0, D, 3 * D)):
            n = i * 3 + j
            copies.append(
                pltpu.make_async_copy(w.at[:, pl.ds(base + i * 256, 256)], buf.at[n], sems.at[n])
            )
    for c in copies:
        c.start()
    normed = norm(tokens[...].astype(jnp.float32)).astype(jnp.bfloat16)

    def proj(n):
        copies[n].wait()
        return silu(jnp.dot(normed, buf[n], preferred_element_type=jnp.float32)).astype(jnp.bfloat16)

    for i in range(4):
        wide = slice(i * 256, (i + 1) * 256)
        gate_out[:, wide] = proj(i * 3)
        v = proj(i * 3 + 1).astype(jnp.float32)
        k = proj(i * 3 + 2).astype(jnp.float32)
        qk = q[:, wide].astype(jnp.float32) * k
        for j in range(2):
            cols = slice(j * HEAD, (j + 1) * HEAD)
            s = jnp.sum(qk[:, cols], axis=1, keepdims=True) * SCALE + self_bias[i * 2 + j]
            self_out[:, i * 256 + j * HEAD : i * 256 + (j + 1) * HEAD] = silu(s) * v[:, cols]
    held.wait()


def rest(tokens, w, q, self_bias, w2):
    return pl.pallas_call(
        rest_kernel,
        out_shape=(
            jax.ShapeDtypeStruct((ROWS, D), jnp.bfloat16),
            jax.ShapeDtypeStruct((ROWS, D), jnp.float32),
            pltpu.VMEM((D, D), jnp.bfloat16),
        ),
        in_specs=[VM, HB, VM, SM, HB],
        out_specs=(VM, VM, VM),
        scratch_shapes=[
            pltpu.VMEM((12, D, 256), jnp.bfloat16),
            pltpu.SemaphoreType.DMA((12,)),
            pltpu.SemaphoreType.DMA,
        ],
        compiler_params=params(20),
        name="project_rest",
    )(
        tokens,
        pltpu.with_memory_space_constraint(w, pltpu.HBM),
        q,
        self_bias,
        pltpu.with_memory_space_constraint(w2, pltpu.HBM),
    )


def by_side(where, body, first, second, width=1):
    even = lax.rem(lax.div(where[0], width), 2) == 0

    @pl.when(even)
    def _():
        body(*first, *second)

    @pl.when(jnp.logical_not(even))
    def _():
        body(*second, *first)


def bundle_kernel(where, own, far_a, far_b, out_a, out_b):
    def body(high, up, low, down):
        up[:QROWS] = own[...]
        up[QROWS : 2 * QROWS] = high[...]
        up[2 * QROWS :] = low[:CUT]
        down[:QROWS] = own[...]
        down[QROWS : 2 * QROWS] = low[...]
        down[2 * QROWS :] = high[QROWS - CUT :]

    by_side(where, body, (far_a, out_a), (far_b, out_b))


def bundle(*args):
    shape = jax.ShapeDtypeStruct((2 * QROWS + CUT, HEAD), jnp.bfloat16)
    return pl.pallas_call(
        bundle_kernel,
        out_shape=(shape, shape),
        in_specs=[SM] + [VM] * 3,
        out_specs=(VM, VM),
        compiler_params=params(12),
        name="bundle_queries",
    )(*args)


def stack_kernel(where, own, far_a, far_b, near_a, near_b, out):
    def body(high, plus, low, minus):
        out[0] = own[...]
        out[5] = low[...]
        out[3] = high[...]
        out[7] = minus[:QROWS]
        out[2] = minus[QROWS : 2 * QROWS]
        out[4, :CUT] = minus[2 * QROWS :]
        out[1] = plus[:QROWS]
        out[6] = plus[QROWS : 2 * QROWS]
        out[4, QROWS - CUT :] = plus[2 * QROWS :]

    by_side(where, body, (far_a, near_a), (far_b, near_b))


def stack(*args):
    return pl.pallas_call(
        stack_kernel,
        out_shape=jax.ShapeDtypeStruct((NZ, QROWS, HEAD), jnp.bfloat16),
        in_specs=[SM] + [VM] * 5,
        out_specs=VM,
        compiler_params=params(12),
        name="stack_queries",
    )(*args)


def table_kernel(where, q_own, q_other, plan, tab, ints, sem):
    o = where[0] * 2 + where[1]
    for i, q in enumerate((q_own, q_other)):
        for s in range(NZ):
            ints[i * NZ + s] = q[s, HALF:].astype(jnp.float32).astype(jnp.int32)[0:8]
    copy = pltpu.make_async_copy(ints.at[:, 0], tab, sem)
    copy.start()
    for i in range(4):
        for b in range(16):
            plan[i, b] = -1
    copy.wait()

    def step(row, carry):
        length = tab[row, 2 * NG * CAP] * 256 + tab[row, 2 * NG * CAP + 1]
        for c in range(CAP):
            slot = tab[row, o * CAP + c]

            @pl.when(slot >= 0)
            def _():
                p = tab[row, NG * CAP + o * CAP + c]
                plan[0, slot] = row
                plan[1, slot] = p
                plan[2, slot] = length - p * BLOCK

        return carry

    lax.fori_loop(0, NG, step, 0)
    budget = FIRST + 3 * where[1]
    for b in range(BLK):
        budget -= (plan[0, b] >= NZ).astype(jnp.int32)
    for b in range(BLK):
        row = plan[0, b]
        mine = (row >= 0) & (row < NZ)
        later = mine & (budget <= 0)
        budget -= mine.astype(jnp.int32)
        plan[3, b] = jnp.where(row < 0, -1, jnp.where(later, 1, 0))


def table(where, q_own, q_other):
    return pl.pallas_call(
        table_kernel,
        out_shape=jax.ShapeDtypeStruct((4, 16), jnp.int32),
        in_specs=[SM, VM, VM],
        out_specs=SM,
        scratch_shapes=[
            pltpu.SMEM((NG, 128), jnp.int32),
            pltpu.VMEM((NG, 8, 128), jnp.int32),
            pltpu.SemaphoreType.DMA,
        ],
        compiler_params=params(12),
        name="read_tables",
    )(where, q_own, q_other)


def attend_blocks(phase, plan, where, bias, pick, blocks, ready, acc):
    h = where[2]
    for b in range(BLK):
        ready(b)

        @pl.when(plan[3, b] == phase)
        def _():
            row = plan[0, b]
            keys = blocks[b, :, 0].reshape(BLOCK, HEAD)
            values = blocks[b, :, 1].reshape(BLOCK, HEAD)
            scores = lax.dot_general(
                pick(row), keys, (((1,), (1,)), ((), ())), preferred_element_type=jnp.float32
            )
            t = scores * (0.5 * SCALE) + bias[h, plan[1, b]] * 0.5
            weights = (t + t * jnp.tanh(t)).astype(jnp.bfloat16)
            acc[row] += jnp.dot(weights, values, preferred_element_type=jnp.float32)


def first_kernel(plan, where, bias, q_own, q_other, kv, own, other, blocks, acc, sems):
    copies = [pltpu.make_async_copy(kv.at[:, :, b], blocks.at[b], sems.at[b]) for b in range(BLK)]
    for c in copies[:2]:
        c.start()
    acc[...] = jnp.zeros_like(acc)
    for c in copies[2:]:
        c.start()

    def pick(row):
        return jnp.where(row < NZ, q_own[lax.rem(row, NZ), :HALF], q_other[lax.rem(row, NZ), :HALF])

    def ready(b):
        copies[b].wait()

        @pl.when((plan[0, b] >= 0) & (plan[2, b] < BLOCK))
        def _():
            values = blocks[b, :, 1].reshape(BLOCK, HEAD)
            token = lax.broadcasted_iota(jnp.int32, (BLOCK, HEAD), 0)
            values = jnp.where(token < plan[2, b], values, jnp.zeros_like(values))
            blocks[b, :, 1] = values.reshape(NM, SLAB, HEAD)

    attend_blocks(0, plan, where, bias, pick, blocks, ready, acc)
    own[...] = acc[:NZ]
    other[...] = acc[NZ:].astype(jnp.bfloat16)


def second_kernel(plan, where, bias, q, blocks, own, out, acc):
    acc[...] = own[...]
    attend_blocks(1, plan, where, bias, lambda row: q[row, :HALF], blocks, lambda b: None, acc)
    out[...] = acc[...].astype(jnp.bfloat16)


def attend_first(plan, where, bias, q_own, q_other, kv):
    return pl.pallas_call(
        first_kernel,
        out_shape=(
            jax.ShapeDtypeStruct((NZ, HALF, HEAD), jnp.float32),
            jax.ShapeDtypeStruct((NZ, HALF, HEAD), jnp.bfloat16),
            jax.ShapeDtypeStruct((BLK, NM, 2, SLAB, HEAD), jnp.bfloat16),
        ),
        in_specs=[SM, SM, SM, VM, VM, HB],
        out_specs=(VM, VM, VM),
        scratch_shapes=[pltpu.VMEM((NG, HALF, HEAD), jnp.float32), pltpu.SemaphoreType.DMA((BLK,))],
        compiler_params=params(20),
        name="attend_first",
    )(plan, where, bias, q_own, q_other, pltpu.with_memory_space_constraint(kv, pltpu.HBM))


def attend_second(plan, where, bias, q, blocks, own):
    return pl.pallas_call(
        second_kernel,
        out_shape=jax.ShapeDtypeStruct((NZ, HALF, HEAD), jnp.bfloat16),
        in_specs=[SM, SM, SM, VM, VM, VM],
        out_specs=VM,
        scratch_shapes=[pltpu.VMEM((NZ, HALF, HEAD), jnp.float32)],
        compiler_params=params(16),
        name="attend_second",
    )(plan, where, bias, q, blocks, own)


def add(*refs):
    total = refs[0].astype(jnp.float32)
    for r in refs[1:]:
        total += r.astype(jnp.float32)
    return total


def far_kernel(where, a, b, out_a, out_b, across):
    def body(up, down):
        up[...] = add(a[3], b[3]).astype(jnp.bfloat16)
        down[...] = add(a[5], b[5]).astype(jnp.bfloat16)

    by_side(where, body, (out_a,), (out_b,))
    across[...] = add(a[4], b[4]).astype(jnp.bfloat16)


def far(*args):
    part = jax.ShapeDtypeStruct((HALF, HEAD), jnp.bfloat16)
    return pl.pallas_call(
        far_kernel,
        out_shape=(part,) * 3,
        in_specs=[SM] + [VM] * 2,
        out_specs=(VM,) * 3,
        compiler_params=params(12),
        name="add_far",
    )(*args)


def side_kernel(where, a, b, after, out_a, out_b):
    def body(up, down):
        up[...] = add(a[1], b[1]).astype(jnp.bfloat16)
        down[...] = add(a[7], b[7]).astype(jnp.bfloat16)

    by_side(where, body, (out_a,), (out_b,))


def side(*args):
    part = jax.ShapeDtypeStruct((HALF, HEAD), jnp.bfloat16)
    return pl.pallas_call(
        side_kernel,
        out_shape=(part, part),
        in_specs=[SM] + [VM] * 3,
        out_specs=(VM,) * 2,
        compiler_params=params(12),
        name="add_side",
    )(*args)


def near_kernel(where, a, b, near_a, near_b, across, out_a, out_b):
    rising = lax.rem(lax.div(where[0], 2), 2) == 0
    goes_up = rising == (where[1] == 1)

    def width(up, down):
        def body(ahead, behind):
            @pl.when(goes_up)
            def _():
                up[...] = add(a[2], b[2], behind[...], across[...]).astype(jnp.bfloat16)
                down[...] = add(a[6], b[6], ahead[...]).astype(jnp.bfloat16)

            @pl.when(jnp.logical_not(goes_up))
            def _():
                up[...] = add(a[2], b[2], behind[...]).astype(jnp.bfloat16)
                down[...] = add(a[6], b[6], ahead[...], across[...]).astype(jnp.bfloat16)

        by_side(where, body, (near_a,), (near_b,))

    by_side(where, width, (out_a,), (out_b,), 2)


def near(*args):
    part = jax.ShapeDtypeStruct((HALF, HEAD), jnp.bfloat16)
    return pl.pallas_call(
        near_kernel,
        out_shape=(part, part),
        in_specs=[SM] + [VM] * 5,
        out_specs=(VM,) * 2,
        compiler_params=params(12),
        name="add_near",
    )(*args)


def total_kernel(own, other, *refs):
    total = add(own[0], other[0], *(r[...] for r in refs[:-1]))
    refs[-1][...] = total.astype(jnp.bfloat16).reshape(HEADS, ROWS, HEAD)


def total(*parts):
    return pl.pallas_call(
        total_kernel,
        out_shape=jax.ShapeDtypeStruct((HEADS, ROWS, HEAD), jnp.bfloat16),
        in_specs=[VM] * 6,
        out_specs=VM,
        compiler_params=params(12),
        name="add_groups",
    )(*parts)


def tail_kernel(hist, self_term, gate, tokens, w, where, count, out):
    attended = jnp.concatenate([hist[h] for h in range(HEADS)], axis=1).astype(jnp.float32) + self_term[...]
    gated = (norm(attended) * gate[...].astype(jnp.float32)).astype(jnp.bfloat16)
    res = jnp.dot(gated, w[...], preferred_element_type=jnp.float32) + tokens[...].astype(jnp.float32)
    row = where[3] * ROWS + lax.broadcasted_iota(jnp.int32, (ROWS, D), 0)
    out[...] = jnp.where(row < count[0], res, 0.0).astype(jnp.bfloat16)


def tail(hist, self_term, gate, tokens, w, where, count):
    return pl.pallas_call(
        tail_kernel,
        out_shape=jax.ShapeDtypeStruct((ROWS, D), jnp.bfloat16),
        in_specs=[VM, VM, VM, VM, VM, SM, SM],
        out_specs=VM,
        compiler_params=params(16),
        name="output",
    )(hist, self_term, gate, tokens, w, where, count)


def move(value, step, width=1):
    pairs = [(i, (i + (-step if i // width % 2 else step)) % NZ) for i in range(NZ)]
    return lax.ppermute(value, "z", pairs)


def cross(value):
    pairs = []
    for i in range(NG):
        step = 2 if (i // 4 + i) % 2 == 0 else -2
        pairs.append((i, (i // 2 + step) % NZ * 2 + i % 2))
    return lax.ppermute(value, G, pairs)


def swap(value):
    return lax.ppermute(value, "core", [(0, 1), (1, 0)])


def local(
    tokens,
    in_weight,
    out_weight,
    history_pool,
    position_bias,
    self_bias,
    history_length,
    candidate_count,
    block_slots,
    block_position,
):
    z, core, m = lax.axis_index("z"), lax.axis_index("core"), lax.axis_index(M)
    where = jnp.stack([z, core, m % HEADS, m]).astype(jnp.int32)
    length = history_length[:, None]
    mine = jnp.concatenate(
        [
            block_slots.reshape(1, NG * CAP),
            block_position.reshape(1, NG * CAP),
            length // 256,
            length % 256,
            jnp.zeros((1, 62), jnp.int32),
        ],
        axis=1,
    ).astype(jnp.bfloat16)
    mine = jnp.broadcast_to(mine, (16, 128))
    q, q_send = query(tokens, in_weight)
    q_mine = lax.all_to_all(q_send, W, split_axis=0, concat_axis=0, tiled=True)
    packed = pack(history_pool, q)
    q_mine, packed = lax.optimization_barrier((q_mine, packed))
    kv = lax.all_to_all(packed, M, split_axis=0, concat_axis=0, tiled=True)
    mine = jnp.concatenate([q_mine.reshape(HALF, HEAD), mine], axis=0)
    far_a, far_b = move(mine, 3), move(mine, -3)
    out_a, out_b = bundle(where, mine, far_a, far_b)
    q_own = stack(where, mine, far_a, far_b, move(out_a, 1), move(out_b, -1))
    q_other = swap(q_own)
    plan = table(where, q_own, q_other)
    gate, self_term, w2 = rest(tokens, in_weight, q, self_bias, out_weight)
    kv, gate, self_term, w2, plan = lax.optimization_barrier((kv, gate, self_term, w2, plan))
    own, other, blocks = attend_first(plan, where, position_bias, q_own, q_other, kv)
    other = swap(other)
    own = attend_second(plan, where, position_bias, q_own, blocks, own)
    out_a, out_b, across = far(where, own, other)
    side_a, side_b = side(where, own, other, out_a)
    side_a, side_b = move(side_a, 1), move(side_b, -1)
    out_a, out_b = near(where, own, other, move(out_a, 1), move(out_b, -1), cross(across))
    hist = total(own, other, side_a, side_b, move(out_a, 2, 2), move(out_b, -2, 2))
    hist = lax.all_to_all(hist, W, split_axis=0, concat_axis=0, tiled=True)
    return tail(hist, self_term, gate, tokens, w2, where, candidate_count)


def solution(mesh):
    names = ("z", "core", "half", "pair", "y")
    fine = Mesh(mesh.devices.reshape(NZ, 2, 2, 2, 4), names)
    placed = (
        P(names, None),
        P(),
        P(),
        P(G, M, None),
        P(),
        P(),
        P(G),
        P(G),
        P(G, None, None),
        P(G, None, None),
    )
    return jax.shard_map(
        local, mesh=fine, in_specs=placed, out_specs=P(names, None), check_vma=False
    )
```

```python
import functools

import jax
import jax.numpy as jnp
from jax import lax
from jax.experimental import pallas as pl
from jax.experimental.pallas import tpu as pltpu
from jax.sharding import Mesh, PartitionSpec as P

D = 1024
HEADS = 8
HEAD = 128
BLOCK = 512
BLK = 14
CAP = 2
NZ = 8
NG = 16
NM = 16
SLAB = 32
ROWS = 64
HALF = 512
QROWS = 528
CUT = 272
FIRST = 9
EPS = 1e-05
SCALE = HEAD**-0.5
G = ("z", "core")
M = ("half", "pair", "y")
W = ("pair", "y")
VM = pl.BlockSpec(memory_space=pltpu.VMEM)
SM = pl.BlockSpec(memory_space=pltpu.SMEM)
HB = pl.BlockSpec(memory_space=pltpu.HBM)


def params(mib):
    return pltpu.CompilerParams(vmem_limit_bytes=mib << 20)


def norm(values):
    center = values - jnp.mean(values, axis=-1, keepdims=True)
    spread = jnp.mean(center * center, axis=-1, keepdims=True)
    return center * lax.rsqrt(spread + EPS)


def silu(v):
    t = 0.5 * v
    return t + t * jnp.tanh(t)


def pack_kernel(pool, after, out):
    for h in range(HEADS):
        for kv in range(2):
            cols = pool[:, :, kv * D + h * HEAD : kv * D + (h + 1) * HEAD]
            for ch in range(2):
                out[ch * HEADS + h, kv] = cols


def pack(pool, after):
    return pl.pallas_call(
        pack_kernel,
        out_shape=jax.ShapeDtypeStruct((NM, 2, BLK, SLAB, HEAD), jnp.bfloat16),
        in_specs=[VM, VM],
        out_specs=VM,
        compiler_params=params(12),
        name="pack_history",
    )(pool, after)


def query_kernel(tokens, w, q_out, send_out, rows, buf, send, sems):
    first = pltpu.make_async_copy(tokens, rows, sems.at[4])
    first.start()
    copies = [
        pltpu.make_async_copy(w.at[:, pl.ds(2 * D + i * 256, 256)], buf.at[i], sems.at[i]) for i in range(4)
    ]
    for c in copies:
        c.start()
    first.wait()
    normed = norm(rows[...].astype(jnp.float32)).astype(jnp.bfloat16)
    moves = []
    for i in range(4):
        copies[i].wait()
        q = silu(jnp.dot(normed, buf[i], preferred_element_type=jnp.float32)).astype(jnp.bfloat16)
        for j in range(2):
            send[i * 2 + j] = q[:, j * HEAD : (j + 1) * HEAD]
        two = pl.ds(i * 2, 2)
        moves.append(pltpu.make_async_copy(send.at[two], send_out.at[two], sems.at[5 + i]))
        moves[i].start()
        q_out[:, i * 256 : (i + 1) * 256] = q
    for c in moves:
        c.wait()


def query(tokens, w):
    return pl.pallas_call(
        query_kernel,
        out_shape=(
            jax.ShapeDtypeStruct((ROWS, D), jnp.bfloat16),
            jax.ShapeDtypeStruct((HEADS, ROWS, HEAD), jnp.bfloat16),
        ),
        in_specs=[HB, HB],
        out_specs=(VM, HB),
        scratch_shapes=[
            pltpu.VMEM((ROWS, D), jnp.bfloat16),
            pltpu.VMEM((4, D, 256), jnp.bfloat16),
            pltpu.VMEM((HEADS, ROWS, HEAD), jnp.bfloat16),
            pltpu.SemaphoreType.DMA((9,)),
        ],
        compiler_params=params(12),
        name="project_query",
    )(pltpu.with_memory_space_constraint(tokens, pltpu.HBM), pltpu.with_memory_space_constraint(w, pltpu.HBM))


def rest_kernel(tokens, w, q, self_bias, w2, gate_out, self_out, w2_out, buf, sems, sem):
    held = pltpu.make_async_copy(w2, w2_out, sem)
    held.start()
    copies = []
    for i in range(4):
        for j, base in enumerate((0, D, 3 * D)):
            n = i * 3 + j
            copies.append(
                pltpu.make_async_copy(w.at[:, pl.ds(base + i * 256, 256)], buf.at[n], sems.at[n])
            )
    for c in copies:
        c.start()
    normed = norm(tokens[...].astype(jnp.float32)).astype(jnp.bfloat16)

    def proj(n):
        copies[n].wait()
        return silu(jnp.dot(normed, buf[n], preferred_element_type=jnp.float32)).astype(jnp.bfloat16)

    for i in range(4):
        wide = slice(i * 256, (i + 1) * 256)
        gate_out[:, wide] = proj(i * 3)
        v = proj(i * 3 + 1).astype(jnp.float32)
        k = proj(i * 3 + 2).astype(jnp.float32)
        qk = q[:, wide].astype(jnp.float32) * k
        for j in range(2):
            cols = slice(j * HEAD, (j + 1) * HEAD)
            s = jnp.sum(qk[:, cols], axis=1, keepdims=True) * SCALE + self_bias[i * 2 + j]
            self_out[:, i * 256 + j * HEAD : i * 256 + (j + 1) * HEAD] = silu(s) * v[:, cols]
    held.wait()


def rest(tokens, w, q, self_bias, w2):
    return pl.pallas_call(
        rest_kernel,
        out_shape=(
            jax.ShapeDtypeStruct((ROWS, D), jnp.bfloat16),
            jax.ShapeDtypeStruct((ROWS, D), jnp.float32),
            pltpu.VMEM((D, D), jnp.bfloat16),
        ),
        in_specs=[VM, HB, VM, SM, HB],
        out_specs=(VM, VM, VM),
        scratch_shapes=[
            pltpu.VMEM((12, D, 256), jnp.bfloat16),
            pltpu.SemaphoreType.DMA((12,)),
            pltpu.SemaphoreType.DMA,
        ],
        compiler_params=params(20),
        name="project_rest",
    )(
        tokens,
        pltpu.with_memory_space_constraint(w, pltpu.HBM),
        q,
        self_bias,
        pltpu.with_memory_space_constraint(w2, pltpu.HBM),
    )


def by_side(where, body, first, second, width=1):
    even = lax.rem(lax.div(where[0], width), 2) == 0

    @pl.when(even)
    def _():
        body(*first, *second)

    @pl.when(jnp.logical_not(even))
    def _():
        body(*second, *first)


def bundle_kernel(where, own, far_a, far_b, out_a, out_b):
    def body(high, up, low, down):
        up[:QROWS] = own[...]
        up[QROWS : 2 * QROWS] = high[...]
        up[2 * QROWS :] = low[:CUT]
        down[:QROWS] = own[...]
        down[QROWS : 2 * QROWS] = low[...]
        down[2 * QROWS :] = high[QROWS - CUT :]

    by_side(where, body, (far_a, out_a), (far_b, out_b))


def bundle(*args):
    shape = jax.ShapeDtypeStruct((2 * QROWS + CUT, HEAD), jnp.bfloat16)
    return pl.pallas_call(
        bundle_kernel,
        out_shape=(shape, shape),
        in_specs=[SM] + [VM] * 3,
        out_specs=(VM, VM),
        compiler_params=params(12),
        name="bundle_queries",
    )(*args)


def stack_kernel(where, own, far_a, far_b, near_a, near_b, out):
    def body(high, plus, low, minus):
        out[0] = own[...]
        out[5] = low[...]
        out[3] = high[...]
        out[7] = minus[:QROWS]
        out[2] = minus[QROWS : 2 * QROWS]
        out[4, :CUT] = minus[2 * QROWS :]
        out[1] = plus[:QROWS]
        out[6] = plus[QROWS : 2 * QROWS]
        out[4, QROWS - CUT :] = plus[2 * QROWS :]

    by_side(where, body, (far_a, near_a), (far_b, near_b))


def stack(*args):
    return pl.pallas_call(
        stack_kernel,
        out_shape=jax.ShapeDtypeStruct((NZ, QROWS, HEAD), jnp.bfloat16),
        in_specs=[SM] + [VM] * 5,
        out_specs=VM,
        compiler_params=params(12),
        name="stack_queries",
    )(*args)


def table_kernel(where, q_own, q_other, plan, tab, ints, sem):
    o = where[0] * 2 + where[1]
    for i, q in enumerate((q_own, q_other)):
        for s in range(NZ):
            ints[i * NZ + s] = q[s, HALF:].astype(jnp.float32).astype(jnp.int32)[0:8]
    copy = pltpu.make_async_copy(ints.at[:, 0], tab, sem)
    copy.start()
    for i in range(4):
        for b in range(16):
            plan[i, b] = -1
    copy.wait()

    def step(row, carry):
        length = tab[row, 2 * NG * CAP] * 256 + tab[row, 2 * NG * CAP + 1]
        for c in range(CAP):
            slot = tab[row, o * CAP + c]

            @pl.when(slot >= 0)
            def _():
                p = tab[row, NG * CAP + o * CAP + c]
                plan[0, slot] = row
                plan[1, slot] = p
                plan[2, slot] = length - p * BLOCK

        return carry

    lax.fori_loop(0, NG, step, 0)
    budget = FIRST + 3 * where[1]
    for b in range(BLK):
        budget -= (plan[0, b] >= NZ).astype(jnp.int32)
    for b in range(BLK):
        row = plan[0, b]
        mine = (row >= 0) & (row < NZ)
        later = mine & (budget <= 0)
        budget -= mine.astype(jnp.int32)
        plan[3, b] = jnp.where(row < 0, -1, jnp.where(later, 1, 0))


def table(where, q_own, q_other):
    return pl.pallas_call(
        table_kernel,
        out_shape=jax.ShapeDtypeStruct((4, 16), jnp.int32),
        in_specs=[SM, VM, VM],
        out_specs=SM,
        scratch_shapes=[
            pltpu.SMEM((NG, 128), jnp.int32),
            pltpu.VMEM((NG, 8, 128), jnp.int32),
            pltpu.SemaphoreType.DMA,
        ],
        compiler_params=params(12),
        name="read_tables",
    )(where, q_own, q_other)


def attend_blocks(phase, plan, where, bias, pick, blocks, ready, acc):
    h = where[2]
    for b in range(BLK):
        ready(b)

        @pl.when(plan[3, b] == phase)
        def _():
            row = plan[0, b]
            keys = blocks[b, :, 0].reshape(BLOCK, HEAD)
            values = blocks[b, :, 1].reshape(BLOCK, HEAD)
            scores = lax.dot_general(
                pick(row), keys, (((1,), (1,)), ((), ())), preferred_element_type=jnp.float32
            )
            t = scores * (0.5 * SCALE) + bias[h, plan[1, b]] * 0.5
            weights = (t + t * jnp.tanh(t)).astype(jnp.bfloat16)
            acc[row] += jnp.dot(weights, values, preferred_element_type=jnp.float32)


def first_kernel(plan, where, bias, q_own, q_other, kv, own, other, blocks, acc, sems):
    copies = [pltpu.make_async_copy(kv.at[:, :, b], blocks.at[b], sems.at[b]) for b in range(BLK)]
    for c in copies[:2]:
        c.start()
    acc[...] = jnp.zeros_like(acc)
    for c in copies[2:]:
        c.start()

    def pick(row):
        return jnp.where(row < NZ, q_own[lax.rem(row, NZ), :HALF], q_other[lax.rem(row, NZ), :HALF])

    def ready(b):
        copies[b].wait()

        @pl.when((plan[0, b] >= 0) & (plan[2, b] < BLOCK))
        def _():
            values = blocks[b, :, 1].reshape(BLOCK, HEAD)
            token = lax.broadcasted_iota(jnp.int32, (BLOCK, HEAD), 0)
            values = jnp.where(token < plan[2, b], values, jnp.zeros_like(values))
            blocks[b, :, 1] = values.reshape(NM, SLAB, HEAD)

    attend_blocks(0, plan, where, bias, pick, blocks, ready, acc)
    own[...] = acc[:NZ]
    other[...] = acc[NZ:].astype(jnp.bfloat16)


def second_kernel(plan, where, bias, q, blocks, own, out, acc):
    acc[...] = own[...]
    attend_blocks(1, plan, where, bias, lambda row: q[row, :HALF], blocks, lambda b: None, acc)
    out[...] = acc[...].astype(jnp.bfloat16)


def attend_first(plan, where, bias, q_own, q_other, kv):
    return pl.pallas_call(
        first_kernel,
        out_shape=(
            jax.ShapeDtypeStruct((NZ, HALF, HEAD), jnp.float32),
            jax.ShapeDtypeStruct((NZ, HALF, HEAD), jnp.bfloat16),
            jax.ShapeDtypeStruct((BLK, NM, 2, SLAB, HEAD), jnp.bfloat16),
        ),
        in_specs=[SM, SM, SM, VM, VM, HB],
        out_specs=(VM, VM, VM),
        scratch_shapes=[pltpu.VMEM((NG, HALF, HEAD), jnp.float32), pltpu.SemaphoreType.DMA((BLK,))],
        compiler_params=params(20),
        name="attend_first",
    )(plan, where, bias, q_own, q_other, pltpu.with_memory_space_constraint(kv, pltpu.HBM))


def attend_second(plan, where, bias, q, blocks, own):
    return pl.pallas_call(
        second_kernel,
        out_shape=jax.ShapeDtypeStruct((NZ, HALF, HEAD), jnp.bfloat16),
        in_specs=[SM, SM, SM, VM, VM, VM],
        out_specs=VM,
        scratch_shapes=[pltpu.VMEM((NZ, HALF, HEAD), jnp.float32)],
        compiler_params=params(16),
        name="attend_second",
    )(plan, where, bias, q, blocks, own)


def add(*refs):
    total = refs[0].astype(jnp.float32)
    for r in refs[1:]:
        total += r.astype(jnp.float32)
    return total


def far_kernel(where, a, b, out_a, out_b, across):
    def body(up, down):
        up[...] = add(a[3], b[3]).astype(jnp.bfloat16)
        down[...] = add(a[5], b[5]).astype(jnp.bfloat16)

    by_side(where, body, (out_a,), (out_b,))
    across[...] = add(a[4], b[4]).astype(jnp.bfloat16)


def far(*args):
    part = jax.ShapeDtypeStruct((HALF, HEAD), jnp.bfloat16)
    return pl.pallas_call(
        far_kernel,
        out_shape=(part,) * 3,
        in_specs=[SM] + [VM] * 2,
        out_specs=(VM,) * 3,
        compiler_params=params(12),
        name="add_far",
    )(*args)


def side_kernel(where, a, b, after, out_a, out_b):
    def body(up, down):
        up[...] = add(a[1], b[1]).astype(jnp.bfloat16)
        down[...] = add(a[7], b[7]).astype(jnp.bfloat16)

    by_side(where, body, (out_a,), (out_b,))


def side(*args):
    part = jax.ShapeDtypeStruct((HALF, HEAD), jnp.bfloat16)
    return pl.pallas_call(
        side_kernel,
        out_shape=(part, part),
        in_specs=[SM] + [VM] * 3,
        out_specs=(VM,) * 2,
        compiler_params=params(12),
        name="add_side",
    )(*args)


def near_kernel(where, a, b, near_a, near_b, across, out_a, out_b):
    rising = lax.rem(lax.div(where[0], 2), 2) == 0
    goes_up = rising == (where[1] == 1)

    def width(up, down):
        def body(ahead, behind):
            @pl.when(goes_up)
            def _():
                up[...] = add(a[2], b[2], behind[...], across[...]).astype(jnp.bfloat16)
                down[...] = add(a[6], b[6], ahead[...]).astype(jnp.bfloat16)

            @pl.when(jnp.logical_not(goes_up))
            def _():
                up[...] = add(a[2], b[2], behind[...]).astype(jnp.bfloat16)
                down[...] = add(a[6], b[6], ahead[...], across[...]).astype(jnp.bfloat16)

        by_side(where, body, (near_a,), (near_b,))

    by_side(where, width, (out_a,), (out_b,), 2)


def near(*args):
    part = jax.ShapeDtypeStruct((HALF, HEAD), jnp.bfloat16)
    return pl.pallas_call(
        near_kernel,
        out_shape=(part, part),
        in_specs=[SM] + [VM] * 5,
        out_specs=(VM,) * 2,
        compiler_params=params(12),
        name="add_near",
    )(*args)


def here_kernel(own, other, side_a, side_b, out):
    out[...] = add(own[0], other[0], side_a[...], side_b[...])


def here_sum(*parts):
    return pl.pallas_call(
        here_kernel,
        out_shape=jax.ShapeDtypeStruct((HALF, HEAD), jnp.float32),
        in_specs=[VM] * 4,
        out_specs=VM,
        compiler_params=params(12),
        name="add_here",
    )(*parts)


def total_kernel(here, a, b, out):
    out[...] = add(here[...], a[...], b[...]).astype(jnp.bfloat16).reshape(HEADS, ROWS, HEAD)


def total(*parts):
    return pl.pallas_call(
        total_kernel,
        out_shape=jax.ShapeDtypeStruct((HEADS, ROWS, HEAD), jnp.bfloat16),
        in_specs=[VM] * 3,
        out_specs=VM,
        compiler_params=params(12),
        name="add_groups",
    )(*parts)


def tail_kernel(hist, self_term, gate, tokens, w, where, count, out):
    attended = jnp.concatenate([hist[h] for h in range(HEADS)], axis=1).astype(jnp.float32) + self_term[...]
    gated = (norm(attended) * gate[...].astype(jnp.float32)).astype(jnp.bfloat16)
    res = jnp.dot(gated, w[...], preferred_element_type=jnp.float32) + tokens[...].astype(jnp.float32)
    row = where[3] * ROWS + lax.broadcasted_iota(jnp.int32, (ROWS, D), 0)
    out[...] = jnp.where(row < count[0], res, 0.0).astype(jnp.bfloat16)


def tail(hist, self_term, gate, tokens, w, where, count):
    return pl.pallas_call(
        tail_kernel,
        out_shape=jax.ShapeDtypeStruct((ROWS, D), jnp.bfloat16),
        in_specs=[VM, VM, VM, VM, VM, SM, SM],
        out_specs=VM,
        compiler_params=params(16),
        name="output",
    )(hist, self_term, gate, tokens, w, where, count)


def move(value, step, width=1):
    pairs = [(i, (i + (-step if i // width % 2 else step)) % NZ) for i in range(NZ)]
    return lax.ppermute(value, "z", pairs)


def cross(value):
    pairs = []
    for i in range(NG):
        step = 2 if (i // 4 + i) % 2 == 0 else -2
        pairs.append((i, (i // 2 + step) % NZ * 2 + i % 2))
    return lax.ppermute(value, G, pairs)


def swap(value):
    return lax.ppermute(value, "core", [(0, 1), (1, 0)])


def local(
    tokens,
    in_weight,
    out_weight,
    history_pool,
    position_bias,
    self_bias,
    history_length,
    candidate_count,
    block_slots,
    block_position,
):
    z, core, m = lax.axis_index("z"), lax.axis_index("core"), lax.axis_index(M)
    where = jnp.stack([z, core, m % HEADS, m]).astype(jnp.int32)
    length = history_length[:, None]
    mine = jnp.concatenate(
        [
            block_slots.reshape(1, NG * CAP),
            block_position.reshape(1, NG * CAP),
            length // 256,
            length % 256,
            jnp.zeros((1, 62), jnp.int32),
        ],
        axis=1,
    ).astype(jnp.bfloat16)
    mine = jnp.broadcast_to(mine, (16, 128))
    q, q_send = query(tokens, in_weight)
    q_mine = lax.all_to_all(q_send, W, split_axis=0, concat_axis=0, tiled=True)
    packed = pack(history_pool, q)
    q_mine, packed = lax.optimization_barrier((q_mine, packed))
    kv = lax.all_to_all(packed, M, split_axis=0, concat_axis=0, tiled=True)
    mine = jnp.concatenate([q_mine.reshape(HALF, HEAD), mine], axis=0)
    far_a, far_b = move(mine, 3), move(mine, -3)
    out_a, out_b = bundle(where, mine, far_a, far_b)
    q_own = stack(where, mine, far_a, far_b, move(out_a, 1), move(out_b, -1))
    q_other = swap(q_own)
    plan = table(where, q_own, q_other)
    gate, self_term, w2 = rest(tokens, in_weight, q, self_bias, out_weight)
    kv, gate, self_term, w2, plan = lax.optimization_barrier((kv, gate, self_term, w2, plan))
    own, other, blocks = attend_first(plan, where, position_bias, q_own, q_other, kv)
    other = swap(other)
    own = attend_second(plan, where, position_bias, q_own, blocks, own)
    out_a, out_b, across = far(where, own, other)
    side_a, side_b = side(where, own, other, out_a)
    side_a, side_b = move(side_a, 1), move(side_b, -1)
    out_a, out_b = near(where, own, other, move(out_a, 1), move(out_b, -1), cross(across))
    hist = total(here_sum(own, other, side_a, side_b), move(out_a, 2, 2), move(out_b, -2, 2))
    hist = lax.all_to_all(hist, W, split_axis=0, concat_axis=0, tiled=True)
    return tail(hist, self_term, gate, tokens, w2, where, candidate_count)


def solution(mesh):
    names = ("z", "core", "half", "pair", "y")
    fine = Mesh(mesh.devices.reshape(NZ, 2, 2, 2, 4), names)
    placed = (
        P(names, None),
        P(),
        P(),
        P(G, M, None),
        P(),
        P(),
        P(G),
        P(G),
        P(G, None, None),
        P(G, None, None),
    )
    return jax.shard_map(
        local, mesh=fine, in_specs=placed, out_specs=P(names, None), check_vma=False
    )
```
